32 devices in a mesh: group: 2 (over x), ctx: 4 (over y, core), exp: 4 (over z).
Axes of the slice: x: 2, y: 2, z: 4, core: 2. Of those that a mesh axis runs over, the one named last changes fastest.
Arguments:
- queries: bfloat16 [1024, 1536], P(('group', 'ctx'), 'exp'), may hold values from -10.5 to 10.5
- keys: bfloat16 [1024, 512], P(('group', 'ctx'), 'exp'), may hold values from -4 to 4
- values: bfloat16 [1024, 512], P(('group', 'ctx'), 'exp'), may hold values from -6 to 6
- residual_in: bfloat16 [1024, 1536], P(('group', 'ctx', 'exp')), may hold values from -6 to 6
- doc_lengths: int32 [4], replicated, may hold values from 1 to 384, 1024 in all
- w_out: bfloat16 [1536, 1536], P('exp', 'group'), may hold values from -0.15625 to 0.15625
- norm_gain: float32 [1536], replicated, may hold values from 0.5 to 1.5
- router: bfloat16 [1536, 16], replicated, may hold values from -0.15625 to 0.15625
- expert_ids: int32 [1024, 6], P(('group', 'ctx', 'exp')), may hold values from 0 to 15, all different within a row; in each aligned block of 32 rows (0 to 31, 32 to 63, ...) at most 18 rows name the same one
- expert_gate_up: bfloat16 [16, 1536, 1024], P(('ctx', 'exp'), 'group'), may hold values from -0.15625 to 0.15625
- expert_down: bfloat16 [16, 1536, 512], P(('ctx', 'exp'), 'group'), may hold values from -0.25 to 0.25
- shared_gate_up: bfloat16 [1536, 2, 1024], P(None, None, 'exp'), may hold values from -0.15625 to 0.15625
- shared_down: bfloat16 [1024, 1536], P('exp'), may hold values from -0.1875 to 0.1875
Outputs:
- hidden_out: bfloat16 [1024, 1536], P(('group', 'ctx', 'exp'))
The draws below stay inside these ranges and needn't reach their ends.
Inputs may be any that keep to these rules, and one draw needn't show every extreme that they name: `doc_lengths`: documents are packed back to back in stream order and one of them has length 384. `expert_ids`: within the 32 rows of one device along group+ctx+exp, no expert is named by more than 18 routes, a bound that some block reaches.
All inputs are finite; a program needn't handle non-finite values.
Results may differ from the reference program's by a relative error of at most 0.015.
Values may be sent and summed in bfloat16 or wider, within the bound.
A program may use at most 64 MiB of HBM per device.

```python
import math
import jax
import jax.numpy as jnp
import numpy as np
from jax import lax

D = 1536
HEADS = 12
KV_HEADS = 4
HEAD = 128
FFE = 512
FFS = 1024
TOP = 6
TOK_DEV = 128
EXPERTS = 16
TOKENS = 1024
TOK_E = 32
LOOK = 4
MAXLEN = 384
DOCS = 4
CAP = 18


def draw_queries(key, part):
    result = jnp.clip(jax.random.normal(jax.random.fold_in(key, 1), (TOKENS, HEADS * HEAD), jnp.float32), -4.0, 4.0)
    return result.astype(jnp.bfloat16)


def draw_keys(key, part):
    result = jnp.clip(jax.random.normal(jax.random.fold_in(key, 2), (TOKENS, KV_HEADS * HEAD), jnp.float32), -4.0, 4.0)
    return result.astype(jnp.bfloat16)


def block_scale(stream_key, extent, shards, smallest, high):
    level, own = 1.0, jax.random.fold_in(stream_key, 6)
    for dim, blocks in shards:
        draws = jnp.exp(jax.random.uniform(jax.random.fold_in(own, dim), (blocks,), jnp.float32, smallest / len(shards), high / len(shards)))
        level = level * jnp.repeat(draws, extent[dim] // blocks).reshape([-1 if axis == dim else 1 for axis in range(len(extent))])
    return level


def split_up(count, total, reach, slope):
    weights = [(1 << 20) // math.isqrt(standing ** slope) + 1 for standing in range(2, count + 1)]
    surplus, holding = total - reach - (count - 1), [1] * (count - 1)
    while surplus > 0:
        candidates = [i for i in range(count - 1) if holding[i] < reach]
        pool, left = sum([weights[i] for i in candidates]), surplus
        for i in candidates:
            addition = min(reach - holding[i], max(1, left * weights[i] // pool), surplus)
            holding[i] = holding[i] + addition
            surplus = surplus - addition
    return np.array([reach] + holding)


def uneven_parts(own_key, amount, total, limit, slope):
    if amount == 2:
        one = jax.random.randint(own_key, (), max(1, total - limit), min(limit, total - 1) + 1)
        return jnp.stack([one, total - one])
    lengths = jnp.asarray(split_up(amount, total, limit, slope), jnp.int32)
    twos = (amount - 1) // 2
    source_of, taker = lengths[1:1 + 2 * twos:2], lengths[2:2 + 2 * twos:2]
    slack = jnp.minimum(source_of - 1, limit - taker)
    shifted = jax.random.randint(jax.random.fold_in(own_key, 1), (twos,), 0, 1 << 20) % (slack + 1)
    lengths = lengths.at[1:1 + 2 * twos:2].set(source_of - shifted).at[2:2 + 2 * twos:2].set(taker + shifted)
    return lengths[jax.random.permutation(jax.random.fold_in(own_key, 2), amount)]


def deal_out(rng, own, number, rows, count, top, limit, slope):
    order = jax.random.permutation(rng, count)
    packed, usual = load_shares(count, rows * top, limit, slope, True), load_shares(count, rows * top, limit, slope, False)
    places = jnp.arange(count)

    def named(lengths, turn):
        used = int((lengths > 0).sum())
        fixed = max(1, used // 4)
        moved = fixed + (places - fixed + turn * (used - fixed)) % max(1, count - fixed)
        return jnp.zeros((count,), jnp.int32).at[order[jnp.where(places < fixed, places, moved)]].set(jnp.asarray(lengths, jnp.int32))

    lengths = jnp.where(number % 4 == 0, named(packed, number // 4), named(usual, number - number // 4 - 1))
    mixed = jax.random.permutation(jax.random.fold_in(own, 3), count)
    donor, taker = mixed[0:count // 2 * 2:2], mixed[1:count // 2 * 2:2]
    slack = jnp.minimum(lengths[donor] - 1, limit - lengths[taker]) // 2
    slack = jnp.where((donor == order[0]) | (taker == order[0]) | (lengths[taker] == 0), 0, jnp.maximum(slack, 0))
    moved = jax.random.randint(jax.random.fold_in(own, 4), (count // 2,), 0, 1 << 20) % (slack + 1)
    lengths = lengths.at[donor].add(-moved).at[taker].add(moved)
    members = jnp.searchsorted(jnp.cumsum(lengths), jnp.arange(rows * top), side="right").astype(jnp.int32)
    listing = members.reshape(top, rows).T
    listing = listing[jax.random.permutation(jax.random.fold_in(own, 1), rows)]
    turn = jax.random.randint(jax.random.fold_in(own, 2), (rows, 1), 0, top)
    return jnp.take_along_axis(listing, (jnp.arange(top)[None, :] + turn) % top, axis=1)


def load_shares(count, total, reach, slope, full):
    portions = [(1 << 20) // math.isqrt(grade ** slope) + 1 for grade in range(1, count + 1)]
    largest = reach if full else min(reach, max(-(-total // count), total * portions[0] // sum(portions)))
    least = 1 if total - largest >= count - 1 else 0
    counts, rest = [largest] + [least] * (count - 1), total - largest - least * (count - 1)
    while rest > 0:
        free = [i for i in range(1, count) if counts[i] < largest] or [i for i in range(1, count) if counts[i] < reach]
        whole, remaining = sum([portions[i] for i in free]), rest
        for i in free:
            extra = min(reach - counts[i], max(1, remaining * portions[i] // whole), rest)
            counts[i] = counts[i] + extra
            rest = rest - extra
    return np.array(counts)


def noise(rng, extent, width, reach, cuts=(), kind=jnp.bfloat16):
    level = block_scale(rng, extent, cuts, -0.22, 0.18) if cuts else 1.0
    entries = jax.random.normal(rng, extent, jnp.float32) * width * level
    return jnp.minimum(jnp.maximum(entries, -reach), reach).astype(kind)


def setup_inputs(seed: int = 0) -> dict:
    seeds = jax.random.split(jax.random.key(seed), 14)
    queries = draw_queries(jax.random.fold_in(seeds[13], 71), 0)
    keys = draw_keys(jax.random.fold_in(seeds[13], 71), 0)
    values = noise(seeds[2], (TOKENS, KV_HEADS * HEAD), 1.0, 6.0, ((0, 8), (1, 4)))
    residual_in = noise(seeds[3], (TOKENS, D), 1.0, 6.0, ((0, 32),))
    doc_lengths = uneven_parts(seeds[4], DOCS, TOKENS, MAXLEN, 2).astype(jnp.int32)
    w_out = noise(seeds[5], (HEADS * HEAD, D), (HEADS * HEAD) ** -0.5, 0.15625, ((0, 4), (1, 2)))
    norm_gain = jnp.clip(1.0 + 0.1 * jax.random.normal(seeds[6], (D,), jnp.float32), 0.5, 1.5)
    router = noise(seeds[7], (D, EXPERTS), D ** -0.5, 0.15625)
    expert_ids_keys = jax.random.split(jax.random.fold_in(seeds[8], 1), TOKENS // TOK_E)
    expert_ids_turns = jax.random.permutation(jax.random.fold_in(seeds[8], 3), TOKENS // TOK_E)
    expert_ids = jax.vmap(lambda own, number: deal_out(jax.random.fold_in(seeds[8], 2), own, number, TOK_E, EXPERTS, TOP, CAP, 2))(expert_ids_keys, expert_ids_turns).reshape((TOKENS, TOP))
    expert_gate_up = noise(seeds[9], (EXPERTS, D, 2 * FFE), D ** -0.5, 0.15625, ((0, 16), (1, 2)))
    expert_down = noise(seeds[10], (EXPERTS, D, FFE), FFE ** -0.5, 0.25, ((0, 16), (1, 2)))
    shared_gate_up = noise(seeds[11], (D, 2, FFS), D ** -0.5, 0.15625, ((2, 4),))
    shared_down = noise(seeds[12], (FFS, D), FFS ** -0.5, 0.1875, ((0, 4),))
    return dict(queries=queries, keys=keys, values=values, residual_in=residual_in, doc_lengths=doc_lengths, w_out=w_out, norm_gain=norm_gain, router=router, expert_ids=expert_ids, expert_gate_up=expert_gate_up, expert_down=expert_down, shared_gate_up=shared_gate_up, shared_down=shared_down)


neg_big = -1e+30

def doc_starts(positions, doc_lengths):
    doc_ends = jnp.cumsum(doc_lengths, dtype=jnp.int32)
    passed = (doc_ends[None, :] <= positions[:, None]).astype(jnp.int32)
    return lax.optimization_barrier(jnp.sum(passed * doc_lengths[None, :], axis=1, dtype=jnp.int32))

def reference(queries, keys, values, residual_in, doc_lengths, w_out, norm_gain, router, expert_ids, expert_gate_up, expert_down, shared_gate_up, shared_down):
    per_kv = HEADS // KV_HEADS
    score_scale = 1.0 / math.sqrt(HEAD)
    block_count = TOKENS // TOK_DEV
    reach_rows = LOOK * TOK_DEV
    pad_rows = (LOOK - 1) * TOK_DEV
    key_pad = jnp.concatenate([jnp.zeros((pad_rows, KV_HEADS * HEAD), keys.dtype), keys], axis=0)
    value_pad = jnp.concatenate([jnp.zeros((pad_rows, KV_HEADS * HEAD), values.dtype), values], axis=0)

    def attend(block_idx):
        first_row = (block_idx * TOK_DEV).astype(jnp.int32)
        query_pos = first_row + jnp.arange(TOK_DEV, dtype=jnp.int32)
        query_start = doc_starts(query_pos, doc_lengths)
        key_pos = first_row - pad_rows + jnp.arange(reach_rows, dtype=jnp.int32)
        query_block = lax.dynamic_slice_in_dim(queries, first_row, TOK_DEV, 0).reshape(TOK_DEV, KV_HEADS, per_kv, HEAD)
        key_block = lax.dynamic_slice_in_dim(key_pad, first_row, reach_rows, 0).reshape(reach_rows, KV_HEADS, HEAD)
        value_block = lax.dynamic_slice_in_dim(value_pad, first_row, reach_rows, 0).reshape(reach_rows, KV_HEADS, HEAD)
        scores = jnp.einsum('tgpd,sgd->gpts', query_block.astype(jnp.float32), key_block.astype(jnp.float32), precision=lax.Precision.HIGHEST) * score_scale
        allowed = (key_pos[None, :] <= query_pos[:, None]) & (key_pos[None, :] >= query_start[:, None])
        scores = jnp.where(allowed, scores, neg_big)
        row_max = lax.optimization_barrier(jnp.max(scores, axis=-1))
        weights = jnp.where(allowed, jnp.exp(scores - row_max[..., None]), 0.0)
        row_sum = lax.optimization_barrier(jnp.sum(weights, axis=-1))
        rounded = lax.optimization_barrier(weights.astype(jnp.bfloat16))
        run_acc = jnp.einsum('gpts,sgd->gptd', rounded.astype(jnp.float32), value_block.astype(jnp.float32), precision=lax.Precision.HIGHEST)
        attended_block = run_acc / row_sum[..., None]
        attended_block = jnp.transpose(attended_block, (2, 0, 1, 3)).reshape(TOK_DEV, HEADS * HEAD)
        return attended_block.astype(jnp.bfloat16)
    attended = lax.map(attend, jnp.arange(block_count, dtype=jnp.int32)).reshape(TOKENS, HEADS * HEAD)
    projected = jnp.dot(attended, w_out, preferred_element_type=jnp.float32)
    stream = (residual_in.astype(jnp.float32) + projected).astype(jnp.bfloat16)
    stream_f = stream.astype(jnp.float32)
    normed = (stream_f * lax.rsqrt(lax.optimization_barrier(jnp.mean(stream_f * stream_f, axis=-1, keepdims=True)) + 1e-05) * norm_gain).astype(jnp.bfloat16)
    logits = jnp.dot(normed, router, preferred_element_type=jnp.float32)
    raw_gates = jax.nn.sigmoid(jnp.take_along_axis(logits, expert_ids, axis=1))
    gate_probs = raw_gates / lax.optimization_barrier(jnp.sum(raw_gates, axis=-1, keepdims=True))
    shared_gate = jnp.dot(normed, shared_gate_up[:, 0, :], preferred_element_type=jnp.float32)
    shared_up = jnp.dot(normed, shared_gate_up[:, 1, :], preferred_element_type=jnp.float32)
    shared_act = (jax.nn.silu(shared_gate) * shared_up).astype(jnp.bfloat16)
    shared_out = jnp.dot(shared_act, shared_down, preferred_element_type=jnp.float32)
    blocks_e = TOKENS // TOK_E
    flat_ids = expert_ids.reshape(blocks_e, TOK_E * TOP)
    one_hot = (flat_ids[..., None] == jnp.arange(EXPERTS, dtype=jnp.int32)[None, None, :]).astype(jnp.int32)
    slot_of = lax.optimization_barrier(jnp.sum((jnp.cumsum(one_hot, axis=1, dtype=jnp.int32) - 1) * one_hot, axis=-1, dtype=jnp.int32))
    block_ids = jnp.arange(blocks_e, dtype=jnp.int32)[:, None]
    token_idx = block_ids * TOK_E + (jnp.arange(TOK_E * TOP, dtype=jnp.int32) // TOP)[None, :]
    block_full = jnp.broadcast_to(block_ids, flat_ids.shape)
    token_table = jnp.full((EXPERTS, blocks_e, CAP), TOKENS, jnp.int32).at[flat_ids, block_full, slot_of].set(token_idx)
    gate_table = jnp.zeros((EXPERTS, blocks_e, CAP), jnp.float32).at[flat_ids, block_full, slot_of].set(gate_probs.reshape(blocks_e, TOK_E * TOP))
    normed_pad = jnp.concatenate([normed, jnp.zeros((1, D), jnp.bfloat16)], axis=0)

    def expert_step(run_acc, inputs):
        rows_idx, row_gates, gate_up, down_rows = inputs
        rows_idx = rows_idx.reshape(-1)
        gathered = normed_pad[rows_idx]
        pre_act = jnp.dot(gathered, gate_up, preferred_element_type=jnp.float32)
        activated = (jax.nn.silu(pre_act[:, :FFE]) * pre_act[:, FFE:]).astype(jnp.bfloat16)
        result = lax.dot_general(activated, down_rows, (((1,), (1,)), ((), ())), preferred_element_type=jnp.float32).astype(jnp.bfloat16)
        run_acc = run_acc.at[rows_idx].add(row_gates.reshape(-1)[:, None] * result.astype(jnp.float32), mode='drop')
        return (run_acc, None)
    routed, unused = lax.scan(expert_step, jnp.zeros((TOKENS, D), jnp.float32), (token_table, gate_table, expert_gate_up, expert_down))
    return (stream_f + shared_out + routed).astype(jnp.bfloat16)
```

```python
import math

import jax
import jax.numpy as jnp
from jax import lax
from jax.sharding import PartitionSpec as P

HEAD = 128


neg_big = -1e30


def passed_along(shard, axis, by):
    length = lax.axis_size(axis)
    pairs = [(i, i + by) for i in range(length) if 0 <= i + by < length]
    return lax.ppermute(shard, axis, pairs)


def doc_starts(positions, doc_lengths):
    order = jnp.arange(doc_lengths.shape[0], dtype=jnp.int32)
    before = (order[None, :] <= order[:, None]).astype(jnp.int32)
    doc_ends = jnp.sum(before * doc_lengths[None, :], axis=1, dtype=jnp.int32)
    passed = (doc_ends[None, :] <= positions[:, None]).astype(jnp.int32)
    return jnp.sum(passed * doc_lengths[None, :], axis=1, dtype=jnp.int32)


def attend_block(soft_state, kv_block, source, query_heads, query_pos, query_start):
    run_max, run_sum, run_acc = soft_state
    rows_dev = kv_block.shape[1]
    key_pos = source * rows_dev + jnp.arange(rows_dev, dtype=jnp.int32)
    allowed = (key_pos[None, :] <= query_pos[:, None]) & (key_pos[None, :] >= query_start[:, None])
    key_heads = kv_block[0].reshape(rows_dev, -1, HEAD)
    value_heads = kv_block[1].reshape(rows_dev, -1, HEAD)
    scores = jnp.einsum(
        "tgpd,sgd->gpts", query_heads, key_heads, preferred_element_type=jnp.float32
    ) * (1.0 / math.sqrt(HEAD))
    scores = jnp.where(allowed, scores, neg_big)
    new_max = jnp.maximum(run_max, jnp.max(scores, axis=-1))
    weights = jnp.where(allowed, jnp.exp(scores - new_max[..., None]), 0.0)
    factor = jnp.exp(run_max - new_max)
    run_sum = run_sum * factor + jnp.sum(weights, axis=-1)
    run_acc = run_acc * factor[..., None] + jnp.einsum(
        "gpts,sgd->gptd",
        weights.astype(jnp.bfloat16),
        value_heads,
        preferred_element_type=jnp.float32,
    )
    return (new_max, run_sum, run_acc)


def visit_block(soft_state, kv_block, source, query_heads, query_pos, query_start):
    rows_dev = kv_block.shape[1]
    useful = (source >= 0) & (source * rows_dev + rows_dev - 1 >= query_start[0])

    def run_block(inner_state):
        return attend_block(inner_state, kv_block, source, query_heads, query_pos, query_start)

    def keep_block(inner_state):
        return inner_state

    return lax.cond(useful, run_block, keep_block, soft_state)


def turned(shard, axis, by):
    length = lax.axis_size(axis)
    return lax.ppermute(shard, axis, [(i, (i + by) % length) for i in range(length)])


def swapped(shard):
    return lax.ppermute(shard, "group", [(0, 1), (1, 0)])


def matmul(rows, weights):
    return jnp.dot(rows, weights, preferred_element_type=jnp.float32).astype(jnp.bfloat16)


def joined(own_first, own, other):
    first = jnp.where(own_first, own, other)
    second = jnp.where(own_first, other, own)
    return jnp.concatenate([first, second], axis=-1)


def summed_from(partial, length, rows, step):
    total = partial[:rows].astype(jnp.float32)
    for by in range(1, length):
        piece = partial[by * rows : (by + 1) * rows]
        total = total + turned(piece, "exp", step * by).astype(jnp.float32)
    return total


def attend_window(kv, first_key, query_heads, query_pos, query_start):
    count = kv.shape[1]
    key_pos = first_key + jnp.arange(count, dtype=jnp.int32)
    allowed = (key_pos[None, :] <= query_pos[:, None]) & (key_pos[None, :] >= query_start[:, None])
    key_heads = kv[0].reshape(count, -1, HEAD)
    value_heads = kv[1].reshape(count, -1, HEAD)
    scores = jnp.einsum(
        "tgpd,sgd->gpts", query_heads, key_heads, preferred_element_type=jnp.float32
    ) * (1.0 / math.sqrt(HEAD))
    scores = jnp.where(allowed, scores, neg_big)
    weights = jnp.where(allowed, jnp.exp(scores - jnp.max(scores, axis=-1, keepdims=True)), 0.0)
    acc = jnp.einsum(
        "gpts,sgd->gptd",
        weights.astype(jnp.bfloat16),
        value_heads,
        preferred_element_type=jnp.float32,
    )
    return acc / jnp.sum(weights, axis=-1, keepdims=True)


def on_device(
    queries,
    keys,
    values,
    residual_in,
    doc_lengths,
    w_out,
    norm_gain,
    router,
    expert_ids,
    expert_gate_up,
    expert_down,
    shared_gate_up,
    shared_down,
):
    rows_dev = queries.shape[0]
    kv_count = keys.shape[1] // HEAD
    per_kv = queries.shape[1] // HEAD // kv_count
    block_count = lax.axis_size("group") * lax.axis_size("ctx")
    look_back = min(32, block_count // 2)
    my_block = lax.axis_index("group") * lax.axis_size("ctx") + lax.axis_index("ctx")
    query_pos = my_block * rows_dev + jnp.arange(rows_dev, dtype=jnp.int32)
    query_start = doc_starts(query_pos, doc_lengths)
    query_heads = queries.reshape(rows_dev, kv_count, per_kv, HEAD)
    init_state = (
        jnp.full((kv_count, per_kv, rows_dev), neg_big, jnp.float32),
        jnp.zeros((kv_count, per_kv, rows_dev), jnp.float32),
        jnp.zeros((kv_count, per_kv, rows_dev, HEAD), jnp.float32),
    )
    group_size = lax.axis_size("group")
    swap = group_size == 2
    kv_own = jnp.stack([keys, values])
    if look_back <= 8:
        blocks = [passed_along(kv_own, ("group", "ctx"), by) for by in range(look_back - 1, 0, -1)]
        kv_all = jnp.concatenate([*blocks, kv_own], axis=1)
    if swap:
        out_other, gate_other, down_other = (
            swapped(w_out), swapped(expert_gate_up), swapped(expert_down)
        )
        own_first = lax.axis_index("group") == 0
    if look_back <= 8:
        first_key = (my_block - (look_back - 1)) * rows_dev
        attended = attend_window(kv_all, first_key, query_heads, query_pos, query_start)
    else:
        soft_state = visit_block(init_state, kv_own, my_block, query_heads, query_pos, query_start)

        def cycle_turn(turn_idx, loop_state):
            moving, inner_state = loop_state
            moving = passed_along(moving, ("group", "ctx"), 1)
            return (
                moving,
                visit_block(
                    inner_state, moving, my_block - turn_idx, query_heads, query_pos, query_start
                ),
            )

        moving, soft_state = lax.fori_loop(1, look_back, cycle_turn, (kv_own, soft_state))
        run_max, run_sum, run_acc = soft_state
        attended = run_acc / run_sum[..., None]
    attended = jnp.transpose(attended, (2, 0, 1, 3)).reshape(rows_dev, -1).astype(jnp.bfloat16)
    exp_size = lax.axis_size("exp")
    exp_me = lax.axis_index("exp")
    tok_e = rows_dev // exp_size
    ahead = [(exp_me + by) % exp_size for by in range(exp_size)]
    rolled = jnp.concatenate(
        [lax.dynamic_slice_in_dim(attended, to * tok_e, tok_e, 0) for to in ahead], axis=0
    )
    if swap:
        partial = joined(own_first, matmul(rolled, w_out), matmul(rolled, out_other))
    else:
        partial = matmul(rolled, lax.all_gather(w_out, "group", axis=1, tiled=True))
    projected = summed_from(partial, exp_size, tok_e, 1)
    stream = (residual_in.astype(jnp.float32) + projected).astype(jnp.bfloat16)
    stream_f = stream.astype(jnp.float32)
    normed = (
        stream_f
        * lax.rsqrt(jnp.mean(stream_f * stream_f, axis=-1, keepdims=True) + 1e-05)
        * norm_gain
    ).astype(jnp.bfloat16)
    expert_count = router.shape[1]
    route_count = expert_ids.shape[1]
    logits = jnp.dot(normed, router, preferred_element_type=jnp.float32)
    chosen = expert_ids[:, :, None] == jnp.arange(expert_count, dtype=jnp.int32)[None, None, :]
    picked_logits = jnp.sum(jnp.where(chosen, logits[:, None, :], 0.0), axis=-1)
    raw_gates = jax.nn.sigmoid(picked_logits)
    gate_probs = raw_gates / jnp.sum(raw_gates, axis=-1, keepdims=True)
    all_normed = jnp.concatenate(
        [normed, *[turned(normed, "exp", by) for by in range(1, exp_size)]], axis=0
    )
    shared_pre = jnp.einsum(
        "td,dkf->tkf", all_normed, shared_gate_up, preferred_element_type=jnp.float32
    )
    shared_act = (jax.nn.silu(shared_pre[:, 0]) * shared_pre[:, 1]).astype(jnp.bfloat16)
    shared_out = summed_from(matmul(shared_act, shared_down), exp_size, tok_e, -1)
    slot_count = max(2, 3 * tok_e * route_count // (2 * expert_count))
    flat_ids = expert_ids.reshape(-1)
    order = jnp.arange(flat_ids.shape[0], dtype=jnp.int32)
    earlier = (flat_ids[None, :] == flat_ids[:, None]) & (order[None, :] < order[:, None])
    slot_of = jnp.sum(earlier.astype(jnp.int32), axis=1, dtype=jnp.int32)
    target = flat_ids * slot_count + slot_of
    placing = (
        jnp.arange(expert_count * slot_count, dtype=jnp.int32)[:, None] == target[None, :]
    ).astype(jnp.bfloat16)
    placing = jnp.sum(placing.reshape(expert_count * slot_count, tok_e, route_count), axis=2)
    model_width = normed.shape[1]
    outgoing = (
        jnp.dot(placing, normed, preferred_element_type=jnp.float32)
        .astype(jnp.bfloat16)
        .reshape(expert_count, slot_count, model_width)
    )
    if not swap:
        gate_up_full = lax.all_gather(expert_gate_up, "group", axis=1, tiled=True)
        down_full = lax.all_gather(expert_down, "group", axis=1, tiled=True)
    hidden_count = expert_down.shape[2]
    local_experts = expert_gate_up.shape[0]
    arrived = lax.all_to_all(outgoing, ("ctx", "exp"), split_axis=0, concat_axis=0, tiled=True)
    sources = arrived.shape[0] // local_experts
    grouped = arrived.reshape(sources, local_experts, arrived.shape[1], arrived.shape[2])
    if swap:
        half = model_width // 2
        mine = lax.dynamic_slice_in_dim(grouped, lax.axis_index("group") * half, half, 3)
        others = lax.dynamic_slice_in_dim(grouped, (1 - lax.axis_index("group")) * half, half, 3)
        pre_act = jnp.einsum(
            "nekd,edf->nekf", mine, expert_gate_up, preferred_element_type=jnp.float32
        ) + jnp.einsum("nekd,edf->nekf", others, gate_other, preferred_element_type=jnp.float32)
    else:
        pre_act = jnp.einsum(
            "nekd,edf->nekf", grouped, gate_up_full, preferred_element_type=jnp.float32
        )
    activated = (jax.nn.silu(pre_act[..., :hidden_count]) * pre_act[..., hidden_count:]).astype(
        jnp.bfloat16
    )
    def down(rows):
        return jnp.einsum(
            "nekf,edf->nekd", activated, rows, preferred_element_type=jnp.float32
        ).astype(jnp.bfloat16)

    if swap:
        result = joined(own_first, down(expert_down), down(down_other))
    else:
        result = down(down_full)
    returned = lax.all_to_all(
        result.reshape(arrived.shape), ("ctx", "exp"), split_axis=0, concat_axis=0, tiled=True
    )
    flat_back = returned.reshape(expert_count * slot_count, model_width)
    fetched = (
        jnp.take(flat_back, target, axis=0)
        .reshape(tok_e, route_count, model_width)
        .astype(jnp.float32)
    )
    routed = jnp.sum(gate_probs[:, :, None] * fetched, axis=1)
    return (stream_f + shared_out + routed).astype(jnp.bfloat16)


def solution(mesh):
    in_specs = (
        P(("group", "ctx"), "exp"),
        P(("group", "ctx"), "exp"),
        P(("group", "ctx"), "exp"),
        P(("group", "ctx", "exp"), None),
        P(),
        P("exp", "group"),
        P(),
        P(),
        P(("group", "ctx", "exp"), None),
        P(("ctx", "exp"), "group", None),
        P(("ctx", "exp"), "group", None),
        P(None, None, "exp"),
        P("exp", None),
    )
    out_specs = P(("group", "ctx", "exp"), None)
    return jax.shard_map(
        on_device, mesh=mesh, in_specs=in_specs, out_specs=out_specs, check_vma=False
    )
```

```python
import math

import jax
import jax.numpy as jnp
from jax import lax
from jax.experimental import pallas as pl
from jax.experimental.pallas import tpu as pltpu
from jax.sharding import PartitionSpec as P

HEAD = 128


neg_big = -1e30


def passed_along(shard, axis, by):
    length = lax.axis_size(axis)
    pairs = [(i, i + by) for i in range(length) if 0 <= i + by < length]
    return lax.ppermute(shard, axis, pairs)


def doc_starts(positions, doc_lengths):
    order = jnp.arange(doc_lengths.shape[0], dtype=jnp.int32)
    before = (order[None, :] <= order[:, None]).astype(jnp.int32)
    doc_ends = jnp.sum(before * doc_lengths[None, :], axis=1, dtype=jnp.int32)
    passed = (doc_ends[None, :] <= positions[:, None]).astype(jnp.int32)
    return jnp.sum(passed * doc_lengths[None, :], axis=1, dtype=jnp.int32)


def attend_block(soft_state, kv_block, source, query_heads, query_pos, query_start):
    run_max, run_sum, run_acc = soft_state
    rows_dev = kv_block.shape[1]
    key_pos = source * rows_dev + jnp.arange(rows_dev, dtype=jnp.int32)
    allowed = (key_pos[None, :] <= query_pos[:, None]) & (key_pos[None, :] >= query_start[:, None])
    key_heads = kv_block[0].reshape(rows_dev, -1, HEAD)
    value_heads = kv_block[1].reshape(rows_dev, -1, HEAD)
    scores = jnp.einsum(
        "tgpd,sgd->gpts", query_heads, key_heads, preferred_element_type=jnp.float32
    ) * (1.0 / math.sqrt(HEAD))
    scores = jnp.where(allowed, scores, neg_big)
    new_max = jnp.maximum(run_max, jnp.max(scores, axis=-1))
    weights = jnp.where(allowed, jnp.exp(scores - new_max[..., None]), 0.0)
    factor = jnp.exp(run_max - new_max)
    run_sum = run_sum * factor + jnp.sum(weights, axis=-1)
    run_acc = run_acc * factor[..., None] + jnp.einsum(
        "gpts,sgd->gptd",
        weights.astype(jnp.bfloat16),
        value_heads,
        preferred_element_type=jnp.float32,
    )
    return (new_max, run_sum, run_acc)


def visit_block(soft_state, kv_block, source, query_heads, query_pos, query_start):
    rows_dev = kv_block.shape[1]
    useful = (source >= 0) & (source * rows_dev + rows_dev - 1 >= query_start[0])

    def run_block(inner_state):
        return attend_block(inner_state, kv_block, source, query_heads, query_pos, query_start)

    def keep_block(inner_state):
        return inner_state

    return lax.cond(useful, run_block, keep_block, soft_state)


def turned(shard, axis, by):
    length = lax.axis_size(axis)
    return lax.ppermute(shard, axis, [(i, (i + by) % length) for i in range(length)])


def swapped(shard):
    return lax.ppermute(shard, "group", [(0, 1), (1, 0)])


def matmul(rows, weights):
    return jnp.dot(rows, weights, preferred_element_type=jnp.float32).astype(jnp.bfloat16)


def joined(own_first, own, other):
    first = jnp.where(own_first, own, other)
    second = jnp.where(own_first, other, own)
    return jnp.concatenate([first, second], axis=-1)


def summed_from(partial, length, rows, step):
    total = partial[:rows].astype(jnp.float32)
    for by in range(1, length):
        piece = partial[by * rows : (by + 1) * rows]
        total = total + turned(piece, "exp", step * by).astype(jnp.float32)
    return total


def attend_window(kv, first_key, query_heads, query_pos, query_start):
    count = kv.shape[1]
    key_pos = first_key + jnp.arange(count, dtype=jnp.int32)
    allowed = (key_pos[None, :] <= query_pos[:, None]) & (key_pos[None, :] >= query_start[:, None])
    key_heads = kv[0].reshape(count, -1, HEAD)
    value_heads = kv[1].reshape(count, -1, HEAD)
    scores = jnp.einsum(
        "tgpd,sgd->gpts", query_heads, key_heads, preferred_element_type=jnp.float32
    ) * (1.0 / math.sqrt(HEAD))
    scores = jnp.where(allowed, scores, neg_big)
    weights = jnp.where(allowed, jnp.exp(scores - jnp.max(scores, axis=-1, keepdims=True)), 0.0)
    acc = jnp.einsum(
        "gpts,sgd->gptd",
        weights.astype(jnp.bfloat16),
        value_heads,
        preferred_element_type=jnp.float32,
    )
    return acc / jnp.sum(weights, axis=-1, keepdims=True)


MESH = pl.DeviceIdType.MESH
LANES = 128
LOW = 64


def remote(src, dst, sends, recvs, at, device):
    return pltpu.make_async_remote_copy(
        src_ref=src,
        dst_ref=dst,
        send_sem=sends.at[at],
        recv_sem=recvs.at[at],
        device_id=device,
        device_id_type=MESH,
    )


def front_kernel(
    lengths, q, k, v, residual, w_own, gain, router, ids, gate_up, down,
    stream, gathered, gate_full, down_full,
    kv, w_other, att, partial, arrived,
    kv_send, kv_recv, sum_send, sum_recv, tok_send, tok_recv, big_send, big_recv, local_sem,
):
    grp, ctx, exp = lax.axis_index("group"), lax.axis_index("ctx"), lax.axis_index("exp")
    block = grp * 4 + ctx

    def at_block(by):
        other = (block + by) % 8
        return (other // 4, other % 4, exp)

    def at_exp(by):
        return (grp, ctx, (exp + by) % 4)

    y_peer = (grp, (ctx + 2) % 4, exp)
    core_peer = (grp, ctx + 1 - 2 * (ctx % 2), exp)
    x_peer = (1 - grp, ctx, exp)
    barrier = pltpu.get_barrier_semaphore()
    for by in range(1, 8):
        pl.semaphore_signal(barrier, inc=1, device_id=at_block(by), device_id_type=MESH)
    for by in range(1, 4):
        pl.semaphore_signal(barrier, inc=1, device_id=at_exp(by), device_id_type=MESH)
    pl.semaphore_wait(barrier, 10)

    kv_copies = []
    for by in (1, 2, 3):
        for which, ref in ((0, k), (1, v)):
            copy = remote(
                ref, kv.at[by - 1, which], kv_send, kv_recv, 2 * (by - 1) + which, at_block(by)
            )
            copy.start()
            kv_copies.append(copy)
    w_copy = remote(w_own, w_other, big_send, big_recv, 0, x_peer)
    w_copy.start()
    half = gate_up.shape[1]
    mine = pl.ds(pl.multiple_of(grp * half, half), half)
    gate_local = pltpu.make_async_copy(gate_up, gate_full.at[:, mine], local_sem.at[0])
    down_local = pltpu.make_async_copy(down, down_full.at[:, mine], local_sem.at[1])
    gate_local.start()
    down_local.start()

    rows = q.shape[0]
    pos = block * rows + lax.broadcasted_iota(jnp.int32, (rows, 1), 0)
    start = jnp.zeros((rows, 1), jnp.int32)
    end = 0
    for doc in range(lengths.shape[0]):
        end = end + lengths[doc]
        start = start + jnp.where(pos >= end, lengths[doc], 0)
    key_pos = (block - 3) * rows + lax.broadcasted_iota(jnp.int32, (rows, 4 * rows), 1)
    allowed = (key_pos <= pos) & (key_pos >= start)
    for copy in kv_copies:
        copy.wait()
    keys = [kv[2, 0], kv[1, 0], kv[0, 0], k[...]]
    vals = jnp.concatenate([kv[2, 1], kv[1, 1], kv[0, 1], v[...]], axis=0)
    keys = jnp.concatenate(keys, axis=0)
    for head in range(q.shape[1] // HEAD):
        cols = pl.ds(head * HEAD, HEAD)
        scores = lax.dot_general(
            q[:, cols], keys, (((1,), (1,)), ((), ())), preferred_element_type=jnp.float32
        ) * (1.0 / math.sqrt(HEAD))
        scores = jnp.where(allowed, scores, neg_big)
        top = jnp.max(scores, axis=-1, keepdims=True)
        weights = jnp.where(allowed, jnp.exp(scores - top), 0.0)
        total = jnp.sum(weights, axis=-1, keepdims=True)
        acc = jnp.dot(
            weights.astype(jnp.bfloat16), vals, preferred_element_type=jnp.float32
        )
        att[:, cols] = (acc / total).astype(jnp.bfloat16)

    w_copy.wait()
    theirs = gate_full.at[:, mine]
    gate_copy = remote(gate_up, theirs, big_send, big_recv, 1, x_peer)
    down_copy = remote(down, down_full.at[:, mine], big_send, big_recv, 2, x_peer)
    gate_copy.start()
    down_copy.start()

    wide = w_own.shape[1]
    own_cols = pl.ds(pl.multiple_of(grp * wide, wide), wide)
    other_cols = pl.ds(pl.multiple_of((1 - grp) * wide, wide), wide)
    tok = residual.shape[0]
    sums = []
    for by in (2, 1, 3, 0):
        piece = att[pl.ds(pl.multiple_of(((exp + by) % 4) * tok, tok), tok), :]
        partial[by, :, own_cols] = jnp.dot(
            piece, w_own[...], preferred_element_type=jnp.float32
        ).astype(jnp.bfloat16)
        partial[by, :, other_cols] = jnp.dot(
            piece, w_other[...], preferred_element_type=jnp.float32
        ).astype(jnp.bfloat16)
        if by:
            copy = remote(
                partial.at[by], arrived.at[by - 1], sum_send, sum_recv, by - 1, at_exp(by)
            )
            copy.start()
            sums.append(copy)
    total = partial[0].astype(jnp.float32)
    for copy in sums:
        copy.wait()
    for by in range(3):
        total = total + arrived[by].astype(jnp.float32)
    held = (residual[...].astype(jnp.float32) + total).astype(jnp.bfloat16)
    stream[...] = held
    wide_f = held.astype(jnp.float32)
    normed = (
        wide_f
        * lax.rsqrt(jnp.mean(wide_f * wide_f, axis=-1, keepdims=True) + 1e-05)
        * gain[...]
    ).astype(jnp.bfloat16)
    width = normed.shape[1]
    logits = jnp.dot(normed, router[...], preferred_element_type=jnp.float32)
    lane = lax.broadcasted_iota(jnp.int32, (tok, LANES), 1)
    expert = jnp.where(lane >= LOW, lane - LOW, lane)
    named = jnp.zeros((tok, LANES), jnp.float32)
    for route in range(ids.shape[1]):
        named = named + jnp.where(ids[:, route : route + 1] == expert, 1.0, 0.0)
    raw = jnp.where(named > 0.0, 1.0 / (1.0 + jnp.exp(-logits)), 0.0)
    sum_raw = jnp.sum(jnp.where(lane < LOW, raw, 0.0), axis=-1, keepdims=True)
    gates = raw / sum_raw
    high = gates.astype(jnp.bfloat16)
    rest = (gates - high.astype(jnp.float32)).astype(jnp.bfloat16)
    gathered[0, :, :width] = normed
    gathered[0, :, width:] = jnp.where(
        lane < LOW, high.astype(jnp.float32), rest.astype(jnp.float32)
    ).astype(jnp.bfloat16)

    def passing(source, target, device):
        copy = remote(gathered.at[source], gathered.at[target], tok_send, tok_recv, target, device)
        copy.start()
        return copy

    first = {by: passing(0, by, at_exp(by)) for by in (2, 1, 3)}
    second, third = {}, []
    for by in (0, 1, 2, 3):
        if by:
            first[by].wait_recv()
        second[by] = passing(by, 8 + by, y_peer)
        third.append(passing(by, 4 + by, core_peer))
    for by in (0, 1, 2, 3):
        second[by].wait_recv()
        third.append(passing(8 + by, 12 + by, core_peer))
    for copy in third:
        copy.wait_recv()
    for copy in [*first.values(), *second.values(), *third]:
        copy.wait_send()
    gate_local.wait()
    down_local.wait()
    gate_copy.wait()
    down_copy.wait()


def back_kernel(
    parts, shared, stream, out,
    one_in, one_sum, two_in, two_sum, three_in,
    one_send, one_recv, two_send, two_recv, three_send, three_recv,
):
    grp, ctx, exp = lax.axis_index("group"), lax.axis_index("ctx"), lax.axis_index("exp")
    y_peer = (grp, (ctx + 2) % 4, exp)
    core_peer = (grp, ctx + 1 - 2 * (ctx % 2), exp)

    def at_exp(by):
        return (grp, ctx, (exp + by) % 4)

    barrier = pltpu.get_barrier_semaphore()
    for peer in (y_peer, core_peer, at_exp(1), at_exp(2), at_exp(3)):
        pl.semaphore_signal(barrier, inc=1, device_id=peer, device_id_type=MESH)
    pl.semaphore_wait(barrier, 5)

    order = (2, 1, 3, 0)
    one = {}
    for far in (1, 0):
        for by in order:
            at = 4 * far + by
            one[at] = remote(
                parts.at[8 * far + 4 + by], one_in.at[at], one_send, one_recv, at, core_peer
            )
            one[at].start()
    two = {}
    for by in order:
        one[4 + by].wait_recv()
        one_sum[by] = (
            parts[8 + by].astype(jnp.float32) + one_in[4 + by].astype(jnp.float32)
        ).astype(jnp.bfloat16)
        two[by] = remote(one_sum.at[by], two_in.at[by], two_send, two_recv, by, y_peer)
        two[by].start()
    three = []
    for by in order:
        one[by].wait_recv()
        near = (
            parts[by].astype(jnp.float32)
            + one_in[by].astype(jnp.float32)
            + shared[by].astype(jnp.float32)
        )
        two[by].wait_recv()
        near = near + two_in[by].astype(jnp.float32)
        if by:
            two_sum[by - 1] = near.astype(jnp.bfloat16)
            copy = remote(
                two_sum.at[by - 1], three_in.at[by - 1], three_send, three_recv, by - 1,
                at_exp(4 - by),
            )
            copy.start()
            three.append(copy)
        else:
            total = near + stream[...].astype(jnp.float32)
    for copy in three:
        copy.wait_recv()
    for by in range(3):
        total = total + three_in[by].astype(jnp.float32)
    out[...] = total.astype(jnp.bfloat16)
    for copy in [*one.values(), *two.values(), *three]:
        copy.wait_send()


def with_kernels(
    queries, keys, values, residual_in, doc_lengths, w_out, norm_gain, router, expert_ids,
    expert_gate_up, expert_down, shared_gate_up, shared_down,
):
    bf = jnp.bfloat16
    tok, width = residual_in.shape
    experts = router.shape[1]
    heads_dev = queries.shape[1]
    rows = queries.shape[0]
    pad = jnp.pad(router, ((0, 0), (0, LOW - experts)))
    vmem, hbm = pl.BlockSpec(memory_space=pltpu.VMEM), pl.BlockSpec(memory_space=pl.ANY)
    smem = pl.BlockSpec(memory_space=pltpu.SMEM)
    dma = pltpu.SemaphoreType.DMA
    up_shape, down_shape = expert_gate_up.shape, expert_down.shape
    stream, gathered, gate_full, down_full = pl.pallas_call(
        front_kernel,
        out_shape=(
            jax.ShapeDtypeStruct((tok, width), bf),
            jax.ShapeDtypeStruct((16, tok, width + LANES), bf),
            jax.ShapeDtypeStruct((up_shape[0], 2 * up_shape[1], up_shape[2]), bf),
            jax.ShapeDtypeStruct((down_shape[0], 2 * down_shape[1], down_shape[2]), bf),
        ),
        in_specs=[smem, *[vmem] * 8, hbm, hbm],
        out_specs=(vmem, vmem, hbm, hbm),
        scratch_shapes=[
            pltpu.VMEM((3, 2, rows, HEAD), bf),
            pltpu.VMEM(w_out.shape, bf),
            pltpu.VMEM((rows, heads_dev), bf),
            pltpu.VMEM((4, tok, width), bf),
            pltpu.VMEM((3, tok, width), bf),
            dma((6,)), dma((6,)), dma((3,)), dma((3,)), dma((16,)), dma((16,)),
            dma((3,)), dma((3,)), dma((2,)),
        ],
        compiler_params=pltpu.CompilerParams(
            collective_id=0, has_side_effects=True, vmem_limit_bytes=24 * 2**20
        ),
    )(
        doc_lengths, queries, keys, values, residual_in, w_out, norm_gain.reshape(1, -1),
        jnp.concatenate([pad, pad], axis=1), expert_ids, expert_gate_up, expert_down,
    )
    tokens = gathered[:, :, :width].reshape(16 * tok, width)
    coded = gathered[:, :, width:].reshape(16 * tok, LANES).astype(jnp.float32)
    gates = coded[:, :LOW] + coded[:, LOW:]
    local = up_shape[0]
    first = (lax.axis_index("ctx") * lax.axis_size("exp") + lax.axis_index("exp")) * local
    hidden = down_shape[2]
    total = jnp.zeros((16 * tok, width), jnp.float32)
    for e in range(local):
        pre = jnp.dot(tokens, gate_full[e], preferred_element_type=jnp.float32)
        act = (jax.nn.silu(pre[:, :hidden]) * pre[:, hidden:]).astype(bf)
        made = lax.dot_general(
            act, down_full[e], (((1,), (1,)), ((), ())), preferred_element_type=jnp.float32
        ).astype(bf)
        is_mine = jnp.arange(LOW, dtype=jnp.int32)[None, :] == first + e
        gate = jnp.sum(jnp.where(is_mine, gates, 0.0), axis=1, keepdims=True)
        total = total + gate * made.astype(jnp.float32)
    near = tokens[: 4 * tok]
    shared_pre = jnp.einsum(
        "td,dkf->tkf", near, shared_gate_up, preferred_element_type=jnp.float32
    )
    shared_act = (jax.nn.silu(shared_pre[:, 0]) * shared_pre[:, 1]).astype(bf)
    shared = matmul(shared_act, shared_down).reshape(4, tok, width)
    return pl.pallas_call(
        back_kernel,
        out_shape=jax.ShapeDtypeStruct((tok, width), bf),
        in_specs=[vmem] * 3,
        out_specs=vmem,
        scratch_shapes=[
            pltpu.VMEM((8, tok, width), bf),
            pltpu.VMEM((4, tok, width), bf),
            pltpu.VMEM((4, tok, width), bf),
            pltpu.VMEM((3, tok, width), bf),
            pltpu.VMEM((3, tok, width), bf),
            dma((8,)), dma((8,)), dma((4,)), dma((4,)), dma((3,)), dma((3,)),
        ],
        compiler_params=pltpu.CompilerParams(
            collective_id=1, has_side_effects=True, vmem_limit_bytes=24 * 2**20
        ),
    )(total.astype(bf).reshape(16, tok, width), shared, stream)


def on_device(
    queries,
    keys,
    values,
    residual_in,
    doc_lengths,
    w_out,
    norm_gain,
    router,
    expert_ids,
    expert_gate_up,
    expert_down,
    shared_gate_up,
    shared_down,
):
    rows_dev = queries.shape[0]
    kv_count = keys.shape[1] // HEAD
    per_kv = queries.shape[1] // HEAD // kv_count
    block_count = lax.axis_size("group") * lax.axis_size("ctx")
    look_back = min(32, block_count // 2)
    my_block = lax.axis_index("group") * lax.axis_size("ctx") + lax.axis_index("ctx")
    query_pos = my_block * rows_dev + jnp.arange(rows_dev, dtype=jnp.int32)
    query_start = doc_starts(query_pos, doc_lengths)
    query_heads = queries.reshape(rows_dev, kv_count, per_kv, HEAD)
    init_state = (
        jnp.full((kv_count, per_kv, rows_dev), neg_big, jnp.float32),
        jnp.zeros((kv_count, per_kv, rows_dev), jnp.float32),
        jnp.zeros((kv_count, per_kv, rows_dev, HEAD), jnp.float32),
    )
    group_size = lax.axis_size("group")
    swap = group_size == 2
    kv_own = jnp.stack([keys, values])
    if look_back <= 8:
        blocks = [passed_along(kv_own, ("group", "ctx"), by) for by in range(look_back - 1, 0, -1)]
        kv_all = jnp.concatenate([*blocks, kv_own], axis=1)
    if swap:
        out_other, gate_other, down_other = (
            swapped(w_out), swapped(expert_gate_up), swapped(expert_down)
        )
        own_first = lax.axis_index("group") == 0
    if look_back <= 8:
        first_key = (my_block - (look_back - 1)) * rows_dev
        attended = attend_window(kv_all, first_key, query_heads, query_pos, query_start)
    else:
        soft_state = visit_block(init_state, kv_own, my_block, query_heads, query_pos, query_start)

        def cycle_turn(turn_idx, loop_state):
            moving, inner_state = loop_state
            moving = passed_along(moving, ("group", "ctx"), 1)
            return (
                moving,
                visit_block(
                    inner_state, moving, my_block - turn_idx, query_heads, query_pos, query_start
                ),
            )

        moving, soft_state = lax.fori_loop(1, look_back, cycle_turn, (kv_own, soft_state))
        run_max, run_sum, run_acc = soft_state
        attended = run_acc / run_sum[..., None]
    attended = jnp.transpose(attended, (2, 0, 1, 3)).reshape(rows_dev, -1).astype(jnp.bfloat16)
    exp_size = lax.axis_size("exp")
    exp_me = lax.axis_index("exp")
    tok_e = rows_dev // exp_size
    ahead = [(exp_me + by) % exp_size for by in range(exp_size)]
    rolled = jnp.concatenate(
        [lax.dynamic_slice_in_dim(attended, to * tok_e, tok_e, 0) for to in ahead], axis=0
    )
    if swap:
        partial = joined(own_first, matmul(rolled, w_out), matmul(rolled, out_other))
    else:
        partial = matmul(rolled, lax.all_gather(w_out, "group", axis=1, tiled=True))
    projected = summed_from(partial, exp_size, tok_e, 1)
    stream = (residual_in.astype(jnp.float32) + projected).astype(jnp.bfloat16)
    stream_f = stream.astype(jnp.float32)
    normed = (
        stream_f
        * lax.rsqrt(jnp.mean(stream_f * stream_f, axis=-1, keepdims=True) + 1e-05)
        * norm_gain
    ).astype(jnp.bfloat16)
    expert_count = router.shape[1]
    route_count = expert_ids.shape[1]
    logits = jnp.dot(normed, router, preferred_element_type=jnp.float32)
    chosen = expert_ids[:, :, None] == jnp.arange(expert_count, dtype=jnp.int32)[None, None, :]
    picked_logits = jnp.sum(jnp.where(chosen, logits[:, None, :], 0.0), axis=-1)
    raw_gates = jax.nn.sigmoid(picked_logits)
    gate_probs = raw_gates / jnp.sum(raw_gates, axis=-1, keepdims=True)
    all_normed = jnp.concatenate(
        [normed, *[turned(normed, "exp", by) for by in range(1, exp_size)]], axis=0
    )
    shared_pre = jnp.einsum(
        "td,dkf->tkf", all_normed, shared_gate_up, preferred_element_type=jnp.float32
    )
    shared_act = (jax.nn.silu(shared_pre[:, 0]) * shared_pre[:, 1]).astype(jnp.bfloat16)
    shared_out = summed_from(matmul(shared_act, shared_down), exp_size, tok_e, -1)
    slot_count = max(2, 3 * tok_e * route_count // (2 * expert_count))
    flat_ids = expert_ids.reshape(-1)
    order = jnp.arange(flat_ids.shape[0], dtype=jnp.int32)
    earlier = (flat_ids[None, :] == flat_ids[:, None]) & (order[None, :] < order[:, None])
    slot_of = jnp.sum(earlier.astype(jnp.int32), axis=1, dtype=jnp.int32)
    target = flat_ids * slot_count + slot_of
    placing = (
        jnp.arange(expert_count * slot_count, dtype=jnp.int32)[:, None] == target[None, :]
    ).astype(jnp.bfloat16)
    placing = jnp.sum(placing.reshape(expert_count * slot_count, tok_e, route_count), axis=2)
    model_width = normed.shape[1]
    outgoing = (
        jnp.dot(placing, normed, preferred_element_type=jnp.float32)
        .astype(jnp.bfloat16)
        .reshape(expert_count, slot_count, model_width)
    )
    if not swap:
        gate_up_full = lax.all_gather(expert_gate_up, "group", axis=1, tiled=True)
        down_full = lax.all_gather(expert_down, "group", axis=1, tiled=True)
    hidden_count = expert_down.shape[2]
    local_experts = expert_gate_up.shape[0]
    arrived = lax.all_to_all(outgoing, ("ctx", "exp"), split_axis=0, concat_axis=0, tiled=True)
    sources = arrived.shape[0] // local_experts
    grouped = arrived.reshape(sources, local_experts, arrived.shape[1], arrived.shape[2])
    if swap:
        half = model_width // 2
        mine = lax.dynamic_slice_in_dim(grouped, lax.axis_index("group") * half, half, 3)
        others = lax.dynamic_slice_in_dim(grouped, (1 - lax.axis_index("group")) * half, half, 3)
        pre_act = jnp.einsum(
            "nekd,edf->nekf", mine, expert_gate_up, preferred_element_type=jnp.float32
        ) + jnp.einsum("nekd,edf->nekf", others, gate_other, preferred_element_type=jnp.float32)
    else:
        pre_act = jnp.einsum(
            "nekd,edf->nekf", grouped, gate_up_full, preferred_element_type=jnp.float32
        )
    activated = (jax.nn.silu(pre_act[..., :hidden_count]) * pre_act[..., hidden_count:]).astype(
        jnp.bfloat16
    )
    def down(rows):
        return jnp.einsum(
            "nekf,edf->nekd", activated, rows, preferred_element_type=jnp.float32
        ).astype(jnp.bfloat16)

    if swap:
        result = joined(own_first, down(expert_down), down(down_other))
    else:
        result = down(down_full)
    returned = lax.all_to_all(
        result.reshape(arrived.shape), ("ctx", "exp"), split_axis=0, concat_axis=0, tiled=True
    )
    flat_back = returned.reshape(expert_count * slot_count, model_width)
    fetched = (
        jnp.take(flat_back, target, axis=0)
        .reshape(tok_e, route_count, model_width)
        .astype(jnp.float32)
    )
    routed = jnp.sum(gate_probs[:, :, None] * fetched, axis=1)
    return (stream_f + shared_out + routed).astype(jnp.bfloat16)


def solution(mesh):
    in_specs = (
        P(("group", "ctx"), "exp"),
        P(("group", "ctx"), "exp"),
        P(("group", "ctx"), "exp"),
        P(("group", "ctx", "exp"), None),
        P(),
        P("exp", "group"),
        P(),
        P(),
        P(("group", "ctx", "exp"), None),
        P(("ctx", "exp"), "group", None),
        P(("ctx", "exp"), "group", None),
        P(None, None, "exp"),
        P("exp", None),
    )
    out_specs = P(("group", "ctx", "exp"), None)
    sizes = (mesh.shape["group"], mesh.shape["ctx"], mesh.shape["exp"])
    body = with_kernels if sizes == (2, 4, 4) else on_device
    return jax.shard_map(
        body, mesh=mesh, in_specs=in_specs, out_specs=out_specs, check_vma=False
    )
```

```python
import math

import jax
import jax.numpy as jnp
from jax import lax
from jax.experimental import pallas as pl
from jax.experimental.pallas import tpu as pltpu
from jax.sharding import PartitionSpec as P

HEAD = 128


neg_big = -1e30


def passed_along(shard, axis, by):
    length = lax.axis_size(axis)
    pairs = [(i, i + by) for i in range(length) if 0 <= i + by < length]
    return lax.ppermute(shard, axis, pairs)


def doc_starts(positions, doc_lengths):
    order = jnp.arange(doc_lengths.shape[0], dtype=jnp.int32)
    before = (order[None, :] <= order[:, None]).astype(jnp.int32)
    doc_ends = jnp.sum(before * doc_lengths[None, :], axis=1, dtype=jnp.int32)
    passed = (doc_ends[None, :] <= positions[:, None]).astype(jnp.int32)
    return jnp.sum(passed * doc_lengths[None, :], axis=1, dtype=jnp.int32)


def attend_block(soft_state, kv_block, source, query_heads, query_pos, query_start):
    run_max, run_sum, run_acc = soft_state
    rows_dev = kv_block.shape[1]
    key_pos = source * rows_dev + jnp.arange(rows_dev, dtype=jnp.int32)
    allowed = (key_pos[None, :] <= query_pos[:, None]) & (key_pos[None, :] >= query_start[:, None])
    key_heads = kv_block[0].reshape(rows_dev, -1, HEAD)
    value_heads = kv_block[1].reshape(rows_dev, -1, HEAD)
    scores = jnp.einsum(
        "tgpd,sgd->gpts", query_heads, key_heads, preferred_element_type=jnp.float32
    ) * (1.0 / math.sqrt(HEAD))
    scores = jnp.where(allowed, scores, neg_big)
    new_max = jnp.maximum(run_max, jnp.max(scores, axis=-1))
    weights = jnp.where(allowed, jnp.exp(scores - new_max[..., None]), 0.0)
    factor = jnp.exp(run_max - new_max)
    run_sum = run_sum * factor + jnp.sum(weights, axis=-1)
    run_acc = run_acc * factor[..., None] + jnp.einsum(
        "gpts,sgd->gptd",
        weights.astype(jnp.bfloat16),
        value_heads,
        preferred_element_type=jnp.float32,
    )
    return (new_max, run_sum, run_acc)


def visit_block(soft_state, kv_block, source, query_heads, query_pos, query_start):
    rows_dev = kv_block.shape[1]
    useful = (source >= 0) & (source * rows_dev + rows_dev - 1 >= query_start[0])

    def run_block(inner_state):
        return attend_block(inner_state, kv_block, source, query_heads, query_pos, query_start)

    def keep_block(inner_state):
        return inner_state

    return lax.cond(useful, run_block, keep_block, soft_state)


def turned(shard, axis, by):
    length = lax.axis_size(axis)
    return lax.ppermute(shard, axis, [(i, (i + by) % length) for i in range(length)])


def swapped(shard):
    return lax.ppermute(shard, "group", [(0, 1), (1, 0)])


def matmul(rows, weights):
    return jnp.dot(rows, weights, preferred_element_type=jnp.float32).astype(jnp.bfloat16)


def joined(own_first, own, other):
    first = jnp.where(own_first, own, other)
    second = jnp.where(own_first, other, own)
    return jnp.concatenate([first, second], axis=-1)


def summed_from(partial, length, rows, step):
    total = partial[:rows].astype(jnp.float32)
    for by in range(1, length):
        piece = partial[by * rows : (by + 1) * rows]
        total = total + turned(piece, "exp", step * by).astype(jnp.float32)
    return total


def attend_window(kv, first_key, query_heads, query_pos, query_start):
    count = kv.shape[1]
    key_pos = first_key + jnp.arange(count, dtype=jnp.int32)
    allowed = (key_pos[None, :] <= query_pos[:, None]) & (key_pos[None, :] >= query_start[:, None])
    key_heads = kv[0].reshape(count, -1, HEAD)
    value_heads = kv[1].reshape(count, -1, HEAD)
    scores = jnp.einsum(
        "tgpd,sgd->gpts", query_heads, key_heads, preferred_element_type=jnp.float32
    ) * (1.0 / math.sqrt(HEAD))
    scores = jnp.where(allowed, scores, neg_big)
    weights = jnp.where(allowed, jnp.exp(scores - jnp.max(scores, axis=-1, keepdims=True)), 0.0)
    acc = jnp.einsum(
        "gpts,sgd->gptd",
        weights.astype(jnp.bfloat16),
        value_heads,
        preferred_element_type=jnp.float32,
    )
    return acc / jnp.sum(weights, axis=-1, keepdims=True)


MESH = pl.DeviceIdType.MESH
LANES = 128
LOW = 64


def remote(src, dst, sends, recvs, at, device):
    return pltpu.make_async_remote_copy(
        src_ref=src,
        dst_ref=dst,
        send_sem=sends.at[at],
        recv_sem=recvs.at[at],
        device_id=device,
        device_id_type=MESH,
    )


def front_kernel(
    lengths, q, k, v, residual, w_own, gain, router, ids, gate_up, down,
    stream, gathered, gate_full, down_full,
    kv, att, att_other, partial, arrived, crossing, crossed, table,
    kv_send, kv_recv, sum_send, sum_recv, tok_send, tok_recv, big_send, big_recv, cross_send, cross_recv,
    local_sem,
):
    grp, ctx, exp = lax.axis_index("group"), lax.axis_index("ctx"), lax.axis_index("exp")
    block = grp * 4 + ctx

    def at_block(by):
        other = (block + by) % 8
        return (other // 4, other % 4, exp)

    def at_exp(by):
        return (grp, ctx, (exp + by) % 4)

    y_peer = (grp, (ctx + 2) % 4, exp)
    core_peer = (grp, ctx + 1 - 2 * (ctx % 2), exp)
    x_peer = (1 - grp, ctx, exp)
    barrier = pltpu.get_barrier_semaphore()
    for by in range(1, 8):
        pl.semaphore_signal(barrier, inc=1, device_id=at_block(by), device_id_type=MESH)
    for by in range(1, 4):
        pl.semaphore_signal(barrier, inc=1, device_id=at_exp(by), device_id_type=MESH)
    pl.semaphore_wait(barrier, 10)

    kv_copies = []
    for by in (1, 2, 3):
        for which, ref in ((0, k), (1, v)):
            copy = remote(
                ref, kv.at[by - 1, which], kv_send, kv_recv, 2 * (by - 1) + which, at_block(by)
            )
            copy.start()
            kv_copies.append(copy)
    half = gate_up.shape[1]
    piece_rows = half // 6
    bulk = []

    def bulk_send(count):
        for _ in range(count):
            at = len(bulk)
            src, full = (gate_up, gate_full) if at < 6 else (down, down_full)
            from_row = (at % 6) * piece_rows
            to_row = pl.multiple_of(grp * half + from_row, piece_rows)
            copy = remote(
                src.at[:, pl.ds(from_row, piece_rows)],
                full.at[:, pl.ds(to_row, piece_rows)],
                big_send, big_recv, at, x_peer,
            )
            copy.start()
            bulk.append(copy)

    bulk_send(3)
    mine = pl.ds(pl.multiple_of(grp * half, half), half)
    gate_local = pltpu.make_async_copy(gate_up, gate_full.at[:, mine], local_sem.at[0])
    down_local = pltpu.make_async_copy(down, down_full.at[:, mine], local_sem.at[1])
    gate_local.start()
    down_local.start()

    rows = q.shape[0]
    pos = block * rows + lax.broadcasted_iota(jnp.int32, (rows, 1), 0)
    start = jnp.zeros((rows, 1), jnp.int32)
    end = 0
    for doc in range(lengths.shape[0]):
        end = end + lengths[doc]
        start = start + jnp.where(pos >= end, lengths[doc], 0)
    key_pos = (block - 3) * rows + lax.broadcasted_iota(jnp.int32, (rows, 4 * rows), 1)
    allowed = (key_pos <= pos) & (key_pos >= start)
    for copy in kv_copies:
        copy.wait()
    keys = [kv[2, 0], kv[1, 0], kv[0, 0], k[...]]
    vals = jnp.concatenate([kv[2, 1], kv[1, 1], kv[0, 1], v[...]], axis=0)
    keys = jnp.concatenate(keys, axis=0)
    for head in range(q.shape[1] // HEAD):
        cols = pl.ds(head * HEAD, HEAD)
        scores = lax.dot_general(
            q[:, cols], keys, (((1,), (1,)), ((), ())), preferred_element_type=jnp.float32
        ) * (1.0 / math.sqrt(HEAD))
        scores = jnp.where(allowed, scores, neg_big)
        top = jnp.max(scores, axis=-1, keepdims=True)
        weights = jnp.where(allowed, jnp.exp(scores - top), 0.0)
        total = jnp.sum(weights, axis=-1, keepdims=True)
        acc = jnp.dot(
            weights.astype(jnp.bfloat16), vals, preferred_element_type=jnp.float32
        )
        att[:, cols] = (acc / total).astype(jnp.bfloat16)

    att_copy = remote(att, att_other, cross_send, cross_recv, 0, x_peer)
    att_copy.start()
    table[...] = jnp.zeros_like(table)
    experts = router.shape[0]
    table[:experts] = router[...]
    table[LOW : LOW + experts] = router[...]
    att_copy.wait()
    bulk_send(1)

    wide = w_own.shape[1]
    own_cols = pl.ds(pl.multiple_of(grp * wide, wide), wide)
    other_cols = pl.ds(pl.multiple_of((1 - grp) * wide, wide), wide)
    tok = residual.shape[0]
    sums = []
    for by in (2, 1, 3, 0):
        rows_at = pl.ds(pl.multiple_of(((exp + by) % 4) * tok, tok), tok)
        piece = jnp.concatenate([att[rows_at, :], att_other[rows_at, :]], axis=0)
        partial[by] = jnp.dot(
            piece, w_own[...], preferred_element_type=jnp.float32
        ).astype(jnp.bfloat16)
        if by:
            copy = remote(
                partial.at[by], arrived.at[by - 1], sum_send, sum_recv, by - 1, at_exp(by)
            )
            copy.start()
            sums.append(copy)
    total = partial[0].astype(jnp.float32)
    for copy in sums:
        copy.wait()
    for by in range(3):
        total = total + arrived[by].astype(jnp.float32)
    crossing[...] = total[tok:].astype(jnp.bfloat16)
    cross_copy = remote(crossing, crossed, cross_send, cross_recv, 1, x_peer)
    cross_copy.start()
    stream[:, own_cols] = (
        residual[:, own_cols].astype(jnp.float32) + total[:tok]
    ).astype(jnp.bfloat16)
    cross_copy.wait()
    bulk_send(8)
    stream[:, other_cols] = (
        residual[:, other_cols].astype(jnp.float32) + crossed[...].astype(jnp.float32)
    ).astype(jnp.bfloat16)
    wide_f = stream[...].astype(jnp.float32)
    normed = (
        wide_f
        * lax.rsqrt(jnp.mean(wide_f * wide_f, axis=-1, keepdims=True) + 1e-05)
        * gain[...].reshape(1, -1)
    ).astype(jnp.bfloat16)
    width = normed.shape[1]
    logits = lax.dot_general(
        normed, table[...], (((1,), (1,)), ((), ())), preferred_element_type=jnp.float32
    )
    lane = lax.broadcasted_iota(jnp.int32, (tok, LANES), 1)
    row = lax.broadcasted_iota(jnp.int32, (LANES, tok), 0)
    expert = jnp.where(row >= LOW, row - LOW, row)
    columns = jnp.zeros((LANES, tok), jnp.float32)
    for route in range(ids.shape[0]):
        columns = columns + jnp.where(ids[route : route + 1, :] == expert, 1.0, 0.0)
    across = lax.broadcasted_iota(jnp.int32, (tok, tok), 0)
    along = lax.broadcasted_iota(jnp.int32, (tok, tok), 1)
    eye = jnp.where(across == along, 1.0, 0.0).astype(jnp.bfloat16)
    named = lax.dot_general(
        eye, columns.astype(jnp.bfloat16), (((1,), (1,)), ((), ())),
        preferred_element_type=jnp.float32,
    )
    raw = jnp.where(named > 0.0, 1.0 / (1.0 + jnp.exp(-logits)), 0.0)
    sum_raw = jnp.sum(jnp.where(lane < LOW, raw, 0.0), axis=-1, keepdims=True)
    gates = raw / sum_raw
    high = gates.astype(jnp.bfloat16)
    rest = (gates - high.astype(jnp.float32)).astype(jnp.bfloat16)
    gathered[0, :, :width] = normed
    gathered[0, :, width:] = jnp.where(
        lane < LOW, high.astype(jnp.float32), rest.astype(jnp.float32)
    ).astype(jnp.bfloat16)

    def passing(source, target, device):
        copy = remote(gathered.at[source], gathered.at[target], tok_send, tok_recv, target, device)
        copy.start()
        return copy

    first = {by: passing(0, by, at_exp(by)) for by in (2, 1, 3)}
    second, third = {}, []
    for by in (0, 1, 2, 3):
        if by:
            first[by].wait_recv()
        second[by] = passing(by, 8 + by, y_peer)
        third.append(passing(by, 4 + by, core_peer))
    for by in (0, 1, 2, 3):
        second[by].wait_recv()
        third.append(passing(8 + by, 12 + by, core_peer))
    for copy in third:
        copy.wait_recv()
    for copy in [*first.values(), *second.values(), *third]:
        copy.wait_send()
    gate_local.wait()
    down_local.wait()
    for copy in bulk:
        copy.wait()


def back_kernel(
    parts, shared, stream, out,
    one_in, one_sum, two_in, two_sum, three_in,
    one_send, one_recv, two_send, two_recv, three_send, three_recv,
):
    grp, ctx, exp = lax.axis_index("group"), lax.axis_index("ctx"), lax.axis_index("exp")
    y_peer = (grp, (ctx + 2) % 4, exp)
    core_peer = (grp, ctx + 1 - 2 * (ctx % 2), exp)

    def at_exp(by):
        return (grp, ctx, (exp + by) % 4)

    barrier = pltpu.get_barrier_semaphore()
    for peer in (y_peer, core_peer, at_exp(1), at_exp(2), at_exp(3)):
        pl.semaphore_signal(barrier, inc=1, device_id=peer, device_id_type=MESH)
    pl.semaphore_wait(barrier, 5)

    order = (2, 1, 3, 0)
    one = {}
    for far in (1, 0):
        for by in order:
            at = 4 * far + by
            one[at] = remote(
                parts.at[8 * far + 4 + by], one_in.at[at], one_send, one_recv, at, core_peer
            )
            one[at].start()
    two = {}
    for by in order:
        one[4 + by].wait_recv()
        one_sum[by] = (
            parts[8 + by].astype(jnp.float32) + one_in[4 + by].astype(jnp.float32)
        ).astype(jnp.bfloat16)
        two[by] = remote(one_sum.at[by], two_in.at[by], two_send, two_recv, by, y_peer)
        two[by].start()
    three = []
    for by in order:
        one[by].wait_recv()
        near = (
            parts[by].astype(jnp.float32)
            + one_in[by].astype(jnp.float32)
            + shared[by].astype(jnp.float32)
        )
        two[by].wait_recv()
        near = near + two_in[by].astype(jnp.float32)
        if by:
            two_sum[by - 1] = near.astype(jnp.bfloat16)
            copy = remote(
                two_sum.at[by - 1], three_in.at[by - 1], three_send, three_recv, by - 1,
                at_exp(4 - by),
            )
            copy.start()
            three.append(copy)
        else:
            total = near + stream[...].astype(jnp.float32)
    for copy in three:
        copy.wait_recv()
    for by in range(3):
        total = total + three_in[by].astype(jnp.float32)
    out[...] = total.astype(jnp.bfloat16)
    for copy in [*one.values(), *two.values(), *three]:
        copy.wait_send()


def with_kernels(
    queries, keys, values, residual_in, doc_lengths, w_out, norm_gain, router, expert_ids,
    expert_gate_up, expert_down, shared_gate_up, shared_down,
):
    bf = jnp.bfloat16
    tok, width = residual_in.shape
    heads_dev = queries.shape[1]
    rows = queries.shape[0]
    vmem, hbm = pl.BlockSpec(memory_space=pltpu.VMEM), pl.BlockSpec(memory_space=pl.ANY)
    smem = pl.BlockSpec(memory_space=pltpu.SMEM)
    dma = pltpu.SemaphoreType.DMA
    up_shape, down_shape = expert_gate_up.shape, expert_down.shape
    stream, gathered, gate_full, down_full = pl.pallas_call(
        front_kernel,
        out_shape=(
            jax.ShapeDtypeStruct((tok, width), bf),
            jax.ShapeDtypeStruct((16, tok, width + LANES), bf),
            jax.ShapeDtypeStruct((up_shape[0], 2 * up_shape[1], up_shape[2]), bf),
            jax.ShapeDtypeStruct((down_shape[0], 2 * down_shape[1], down_shape[2]), bf),
        ),
        in_specs=[smem, *[vmem] * 8, hbm, hbm],
        out_specs=(vmem, vmem, hbm, hbm),
        scratch_shapes=[
            pltpu.VMEM((3, 2, rows, HEAD), bf),
            pltpu.VMEM((rows, heads_dev), bf),
            pltpu.VMEM((rows, heads_dev), bf),
            pltpu.VMEM((4, 2 * tok, width // 2), bf),
            pltpu.VMEM((3, 2 * tok, width // 2), bf),
            pltpu.VMEM((tok, width // 2), bf),
            pltpu.VMEM((tok, width // 2), bf),
            pltpu.VMEM((LANES, width), bf),
            dma((6,)), dma((6,)), dma((3,)), dma((3,)), dma((16,)), dma((16,)),
            dma((12,)), dma((12,)), dma((2,)), dma((2,)), dma((2,)),
        ],
        compiler_params=pltpu.CompilerParams(
            collective_id=0, has_side_effects=True, vmem_limit_bytes=24 * 2**20
        ),
    )(
        doc_lengths, queries, keys, values, residual_in, w_out, norm_gain,
        router.T, expert_ids.T, expert_gate_up, expert_down,
    )
    tokens = gathered[:, :, :width].reshape(16 * tok, width)
    coded = gathered[:, :, width:].reshape(16 * tok, LANES).astype(jnp.float32)
    gates = coded[:, :LOW] + coded[:, LOW:]
    local = up_shape[0]
    first = (lax.axis_index("ctx") * lax.axis_size("exp") + lax.axis_index("exp")) * local
    hidden = down_shape[2]
    total = jnp.zeros((16 * tok, width), jnp.float32)
    for e in range(local):
        pre = jnp.dot(tokens, gate_full[e], preferred_element_type=jnp.float32)
        act = (jax.nn.silu(pre[:, :hidden]) * pre[:, hidden:]).astype(bf)
        made = lax.dot_general(
            act, down_full[e], (((1,), (1,)), ((), ())), preferred_element_type=jnp.float32
        ).astype(bf)
        is_mine = jnp.arange(LOW, dtype=jnp.int32)[None, :] == first + e
        gate = jnp.sum(jnp.where(is_mine, gates, 0.0), axis=1, keepdims=True)
        total = total + gate * made.astype(jnp.float32)
    near = tokens[: 4 * tok]
    shared_pre = jnp.einsum(
        "td,dkf->tkf", near, shared_gate_up, preferred_element_type=jnp.float32
    )
    shared_act = (jax.nn.silu(shared_pre[:, 0]) * shared_pre[:, 1]).astype(bf)
    shared = matmul(shared_act, shared_down).reshape(4, tok, width)
    return pl.pallas_call(
        back_kernel,
        out_shape=jax.ShapeDtypeStruct((tok, width), bf),
        in_specs=[vmem] * 3,
        out_specs=vmem,
        scratch_shapes=[
            pltpu.VMEM((8, tok, width), bf),
            pltpu.VMEM((4, tok, width), bf),
            pltpu.VMEM((4, tok, width), bf),
            pltpu.VMEM((3, tok, width), bf),
            pltpu.VMEM((3, tok, width), bf),
            dma((8,)), dma((8,)), dma((4,)), dma((4,)), dma((3,)), dma((3,)),
        ],
        compiler_params=pltpu.CompilerParams(
            collective_id=1, has_side_effects=True, vmem_limit_bytes=24 * 2**20
        ),
    )(total.astype(bf).reshape(16, tok, width), shared, stream)


def on_device(
    queries,
    keys,
    values,
    residual_in,
    doc_lengths,
    w_out,
    norm_gain,
    router,
    expert_ids,
    expert_gate_up,
    expert_down,
    shared_gate_up,
    shared_down,
):
    rows_dev = queries.shape[0]
    kv_count = keys.shape[1] // HEAD
    per_kv = queries.shape[1] // HEAD // kv_count
    block_count = lax.axis_size("group") * lax.axis_size("ctx")
    look_back = min(32, block_count // 2)
    my_block = lax.axis_index("group") * lax.axis_size("ctx") + lax.axis_index("ctx")
    query_pos = my_block * rows_dev + jnp.arange(rows_dev, dtype=jnp.int32)
    query_start = doc_starts(query_pos, doc_lengths)
    query_heads = queries.reshape(rows_dev, kv_count, per_kv, HEAD)
    init_state = (
        jnp.full((kv_count, per_kv, rows_dev), neg_big, jnp.float32),
        jnp.zeros((kv_count, per_kv, rows_dev), jnp.float32),
        jnp.zeros((kv_count, per_kv, rows_dev, HEAD), jnp.float32),
    )
    group_size = lax.axis_size("group")
    swap = group_size == 2
    kv_own = jnp.stack([keys, values])
    if look_back <= 8:
        blocks = [passed_along(kv_own, ("group", "ctx"), by) for by in range(look_back - 1, 0, -1)]
        kv_all = jnp.concatenate([*blocks, kv_own], axis=1)
    if swap:
        out_other, gate_other, down_other = (
            swapped(w_out), swapped(expert_gate_up), swapped(expert_down)
        )
        own_first = lax.axis_index("group") == 0
    if look_back <= 8:
        first_key = (my_block - (look_back - 1)) * rows_dev
        attended = attend_window(kv_all, first_key, query_heads, query_pos, query_start)
    else:
        soft_state = visit_block(init_state, kv_own, my_block, query_heads, query_pos, query_start)

        def cycle_turn(turn_idx, loop_state):
            moving, inner_state = loop_state
            moving = passed_along(moving, ("group", "ctx"), 1)
            return (
                moving,
                visit_block(
                    inner_state, moving, my_block - turn_idx, query_heads, query_pos, query_start
                ),
            )

        moving, soft_state = lax.fori_loop(1, look_back, cycle_turn, (kv_own, soft_state))
        run_max, run_sum, run_acc = soft_state
        attended = run_acc / run_sum[..., None]
    attended = jnp.transpose(attended, (2, 0, 1, 3)).reshape(rows_dev, -1).astype(jnp.bfloat16)
    exp_size = lax.axis_size("exp")
    exp_me = lax.axis_index("exp")
    tok_e = rows_dev // exp_size
    ahead = [(exp_me + by) % exp_size for by in range(exp_size)]
    rolled = jnp.concatenate(
        [lax.dynamic_slice_in_dim(attended, to * tok_e, tok_e, 0) for to in ahead], axis=0
    )
    if swap:
        partial = joined(own_first, matmul(rolled, w_out), matmul(rolled, out_other))
    else:
        partial = matmul(rolled, lax.all_gather(w_out, "group", axis=1, tiled=True))
    projected = summed_from(partial, exp_size, tok_e, 1)
    stream = (residual_in.astype(jnp.float32) + projected).astype(jnp.bfloat16)
    stream_f = stream.astype(jnp.float32)
    normed = (
        stream_f
        * lax.rsqrt(jnp.mean(stream_f * stream_f, axis=-1, keepdims=True) + 1e-05)
        * norm_gain
    ).astype(jnp.bfloat16)
    expert_count = router.shape[1]
    route_count = expert_ids.shape[1]
    logits = jnp.dot(normed, router, preferred_element_type=jnp.float32)
    chosen = expert_ids[:, :, None] == jnp.arange(expert_count, dtype=jnp.int32)[None, None, :]
    picked_logits = jnp.sum(jnp.where(chosen, logits[:, None, :], 0.0), axis=-1)
    raw_gates = jax.nn.sigmoid(picked_logits)
    gate_probs = raw_gates / jnp.sum(raw_gates, axis=-1, keepdims=True)
    all_normed = jnp.concatenate(
        [normed, *[turned(normed, "exp", by) for by in range(1, exp_size)]], axis=0
    )
    shared_pre = jnp.einsum(
        "td,dkf->tkf", all_normed, shared_gate_up, preferred_element_type=jnp.float32
    )
    shared_act = (jax.nn.silu(shared_pre[:, 0]) * shared_pre[:, 1]).astype(jnp.bfloat16)
    shared_out = summed_from(matmul(shared_act, shared_down), exp_size, tok_e, -1)
    slot_count = max(2, 3 * tok_e * route_count // (2 * expert_count))
    flat_ids = expert_ids.reshape(-1)
    order = jnp.arange(flat_ids.shape[0], dtype=jnp.int32)
    earlier = (flat_ids[None, :] == flat_ids[:, None]) & (order[None, :] < order[:, None])
    slot_of = jnp.sum(earlier.astype(jnp.int32), axis=1, dtype=jnp.int32)
    target = flat_ids * slot_count + slot_of
    placing = (
        jnp.arange(expert_count * slot_count, dtype=jnp.int32)[:, None] == target[None, :]
    ).astype(jnp.bfloat16)
    placing = jnp.sum(placing.reshape(expert_count * slot_count, tok_e, route_count), axis=2)
    model_width = normed.shape[1]
    outgoing = (
        jnp.dot(placing, normed, preferred_element_type=jnp.float32)
        .astype(jnp.bfloat16)
        .reshape(expert_count, slot_count, model_width)
    )
    if not swap:
        gate_up_full = lax.all_gather(expert_gate_up, "group", axis=1, tiled=True)
        down_full = lax.all_gather(expert_down, "group", axis=1, tiled=True)
    hidden_count = expert_down.shape[2]
    local_experts = expert_gate_up.shape[0]
    arrived = lax.all_to_all(outgoing, ("ctx", "exp"), split_axis=0, concat_axis=0, tiled=True)
    sources = arrived.shape[0] // local_experts
    grouped = arrived.reshape(sources, local_experts, arrived.shape[1], arrived.shape[2])
    if swap:
        half = model_width // 2
        mine = lax.dynamic_slice_in_dim(grouped, lax.axis_index("group") * half, half, 3)
        others = lax.dynamic_slice_in_dim(grouped, (1 - lax.axis_index("group")) * half, half, 3)
        pre_act = jnp.einsum(
            "nekd,edf->nekf", mine, expert_gate_up, preferred_element_type=jnp.float32
        ) + jnp.einsum("nekd,edf->nekf", others, gate_other, preferred_element_type=jnp.float32)
    else:
        pre_act = jnp.einsum(
            "nekd,edf->nekf", grouped, gate_up_full, preferred_element_type=jnp.float32
        )
    activated = (jax.nn.silu(pre_act[..., :hidden_count]) * pre_act[..., hidden_count:]).astype(
        jnp.bfloat16
    )
    def down(rows):
        return jnp.einsum(
            "nekf,edf->nekd", activated, rows, preferred_element_type=jnp.float32
        ).astype(jnp.bfloat16)

    if swap:
        result = joined(own_first, down(expert_down), down(down_other))
    else:
        result = down(down_full)
    returned = lax.all_to_all(
        result.reshape(arrived.shape), ("ctx", "exp"), split_axis=0, concat_axis=0, tiled=True
    )
    flat_back = returned.reshape(expert_count * slot_count, model_width)
    fetched = (
        jnp.take(flat_back, target, axis=0)
        .reshape(tok_e, route_count, model_width)
        .astype(jnp.float32)
    )
    routed = jnp.sum(gate_probs[:, :, None] * fetched, axis=1)
    return (stream_f + shared_out + routed).astype(jnp.bfloat16)


def solution(mesh):
    in_specs = (
        P(("group", "ctx"), "exp"),
        P(("group", "ctx"), "exp"),
        P(("group", "ctx"), "exp"),
        P(("group", "ctx", "exp"), None),
        P(),
        P("exp", "group"),
        P(),
        P(),
        P(("group", "ctx", "exp"), None),
        P(("ctx", "exp"), "group", None),
        P(("ctx", "exp"), "group", None),
        P(None, None, "exp"),
        P("exp", None),
    )
    out_specs = P(("group", "ctx", "exp"), None)
    sizes = (mesh.shape["group"], mesh.shape["ctx"], mesh.shape["exp"])
    body = with_kernels if sizes == (2, 4, 4) else on_device
    return jax.shard_map(
        body, mesh=mesh, in_specs=in_specs, out_specs=out_specs, check_vma=False
    )
```

```python
import math

import jax
import jax.numpy as jnp
from jax import lax
from jax.experimental import pallas as pl
from jax.experimental.pallas import tpu as pltpu
from jax.sharding import PartitionSpec as P

HEAD = 128


neg_big = -1e30


def passed_along(shard, axis, by):
    length = lax.axis_size(axis)
    pairs = [(i, i + by) for i in range(length) if 0 <= i + by < length]
    return lax.ppermute(shard, axis, pairs)


def doc_starts(positions, doc_lengths):
    order = jnp.arange(doc_lengths.shape[0], dtype=jnp.int32)
    before = (order[None, :] <= order[:, None]).astype(jnp.int32)
    doc_ends = jnp.sum(before * doc_lengths[None, :], axis=1, dtype=jnp.int32)
    passed = (doc_ends[None, :] <= positions[:, None]).astype(jnp.int32)
    return jnp.sum(passed * doc_lengths[None, :], axis=1, dtype=jnp.int32)


def attend_block(soft_state, kv_block, source, query_heads, query_pos, query_start):
    run_max, run_sum, run_acc = soft_state
    rows_dev = kv_block.shape[1]
    key_pos = source * rows_dev + jnp.arange(rows_dev, dtype=jnp.int32)
    allowed = (key_pos[None, :] <= query_pos[:, None]) & (key_pos[None, :] >= query_start[:, None])
    key_heads = kv_block[0].reshape(rows_dev, -1, HEAD)
    value_heads = kv_block[1].reshape(rows_dev, -1, HEAD)
    scores = jnp.einsum(
        "tgpd,sgd->gpts", query_heads, key_heads, preferred_element_type=jnp.float32
    ) * (1.0 / math.sqrt(HEAD))
    scores = jnp.where(allowed, scores, neg_big)
    new_max = jnp.maximum(run_max, jnp.max(scores, axis=-1))
    weights = jnp.where(allowed, jnp.exp(scores - new_max[..., None]), 0.0)
    factor = jnp.exp(run_max - new_max)
    run_sum = run_sum * factor + jnp.sum(weights, axis=-1)
    run_acc = run_acc * factor[..., None] + jnp.einsum(
        "gpts,sgd->gptd",
        weights.astype(jnp.bfloat16),
        value_heads,
        preferred_element_type=jnp.float32,
    )
    return (new_max, run_sum, run_acc)


def visit_block(soft_state, kv_block, source, query_heads, query_pos, query_start):
    rows_dev = kv_block.shape[1]
    useful = (source >= 0) & (source * rows_dev + rows_dev - 1 >= query_start[0])

    def run_block(inner_state):
        return attend_block(inner_state, kv_block, source, query_heads, query_pos, query_start)

    def keep_block(inner_state):
        return inner_state

    return lax.cond(useful, run_block, keep_block, soft_state)


def turned(shard, axis, by):
    length = lax.axis_size(axis)
    return lax.ppermute(shard, axis, [(i, (i + by) % length) for i in range(length)])


def swapped(shard):
    return lax.ppermute(shard, "group", [(0, 1), (1, 0)])


def matmul(rows, weights):
    return jnp.dot(rows, weights, preferred_element_type=jnp.float32).astype(jnp.bfloat16)


def joined(own_first, own, other):
    first = jnp.where(own_first, own, other)
    second = jnp.where(own_first, other, own)
    return jnp.concatenate([first, second], axis=-1)


def summed_from(partial, length, rows, step):
    total = partial[:rows].astype(jnp.float32)
    for by in range(1, length):
        piece = partial[by * rows : (by + 1) * rows]
        total = total + turned(piece, "exp", step * by).astype(jnp.float32)
    return total


def attend_window(kv, first_key, query_heads, query_pos, query_start):
    count = kv.shape[1]
    key_pos = first_key + jnp.arange(count, dtype=jnp.int32)
    allowed = (key_pos[None, :] <= query_pos[:, None]) & (key_pos[None, :] >= query_start[:, None])
    key_heads = kv[0].reshape(count, -1, HEAD)
    value_heads = kv[1].reshape(count, -1, HEAD)
    scores = jnp.einsum(
        "tgpd,sgd->gpts", query_heads, key_heads, preferred_element_type=jnp.float32
    ) * (1.0 / math.sqrt(HEAD))
    scores = jnp.where(allowed, scores, neg_big)
    weights = jnp.where(allowed, jnp.exp(scores - jnp.max(scores, axis=-1, keepdims=True)), 0.0)
    acc = jnp.einsum(
        "gpts,sgd->gptd",
        weights.astype(jnp.bfloat16),
        value_heads,
        preferred_element_type=jnp.float32,
    )
    return acc / jnp.sum(weights, axis=-1, keepdims=True)


MESH = pl.DeviceIdType.MESH
LANES = 128
LOW = 64


def remote(src, dst, sends, recvs, at, device):
    return pltpu.make_async_remote_copy(
        src_ref=src,
        dst_ref=dst,
        send_sem=sends.at[at],
        recv_sem=recvs.at[at],
        device_id=device,
        device_id_type=MESH,
    )


def front_kernel(
    lengths, q, k, v, residual, w_own, gain, router, ids, gate_up, down,
    stream, gathered, gate_full, down_full,
    kv, att, att_other, partial, arrived, crossing, crossed, table,
    kv_send, kv_recv, sum_send, sum_recv, tok_send, tok_recv, big_send, big_recv, cross_send, cross_recv,
    local_sem,
):
    grp, ctx, exp = lax.axis_index("group"), lax.axis_index("ctx"), lax.axis_index("exp")
    block = grp * 4 + ctx

    def at_block(by):
        other = (block + by) % 8
        return (other // 4, other % 4, exp)

    def at_exp(by):
        return (grp, ctx, (exp + by) % 4)

    y_peer = (grp, (ctx + 2) % 4, exp)
    core_peer = (grp, ctx + 1 - 2 * (ctx % 2), exp)
    x_peer = (1 - grp, ctx, exp)
    barrier = pltpu.get_barrier_semaphore()
    for by in range(1, 8):
        pl.semaphore_signal(barrier, inc=1, device_id=at_block(by), device_id_type=MESH)
    for by in range(1, 4):
        pl.semaphore_signal(barrier, inc=1, device_id=at_exp(by), device_id_type=MESH)
    pl.semaphore_wait(barrier, 10)

    kv_copies = []
    for by in (1, 2, 3):
        for which, ref in ((0, k), (1, v)):
            copy = remote(
                ref, kv.at[by - 1, which], kv_send, kv_recv, 2 * (by - 1) + which, at_block(by)
            )
            copy.start()
            kv_copies.append(copy)
    half = gate_up.shape[1]
    piece_rows = half // 6
    bulk = []

    def bulk_send(count):
        for _ in range(count):
            at = len(bulk)
            src, full = (gate_up, gate_full) if at < 6 else (down, down_full)
            from_row = (at % 6) * piece_rows
            to_row = pl.multiple_of(grp * half + from_row, piece_rows)
            copy = remote(
                src.at[:, pl.ds(from_row, piece_rows)],
                full.at[:, pl.ds(to_row, piece_rows)],
                big_send, big_recv, at, x_peer,
            )
            copy.start()
            bulk.append(copy)

    bulk_send(3)
    mine = pl.ds(pl.multiple_of(grp * half, half), half)
    gate_local = pltpu.make_async_copy(gate_up, gate_full.at[:, mine], local_sem.at[0])
    down_local = pltpu.make_async_copy(down, down_full.at[:, mine], local_sem.at[1])
    gate_local.start()
    down_local.start()

    rows = q.shape[0]
    pos = block * rows + lax.broadcasted_iota(jnp.int32, (rows, 1), 0)
    start = jnp.zeros((rows, 1), jnp.int32)
    end = 0
    for doc in range(lengths.shape[0]):
        end = end + lengths[doc]
        start = start + jnp.where(pos >= end, lengths[doc], 0)
    key_pos = (block - 3) * rows + lax.broadcasted_iota(jnp.int32, (rows, 4 * rows), 1)
    allowed = (key_pos <= pos) & (key_pos >= start)
    for copy in kv_copies:
        copy.wait()
    keys = [kv[2, 0], kv[1, 0], kv[0, 0], k[...]]
    vals = jnp.concatenate([kv[2, 1], kv[1, 1], kv[0, 1], v[...]], axis=0)
    keys = jnp.concatenate(keys, axis=0)
    for head in range(q.shape[1] // HEAD):
        cols = pl.ds(head * HEAD, HEAD)
        scores = lax.dot_general(
            q[:, cols], keys, (((1,), (1,)), ((), ())), preferred_element_type=jnp.float32
        ) * (1.0 / math.sqrt(HEAD))
        scores = jnp.where(allowed, scores, neg_big)
        top = jnp.max(scores, axis=-1, keepdims=True)
        weights = jnp.where(allowed, jnp.exp(scores - top), 0.0)
        total = jnp.sum(weights, axis=-1, keepdims=True)
        acc = jnp.dot(
            weights.astype(jnp.bfloat16), vals, preferred_element_type=jnp.float32
        )
        att[:, cols] = (acc / total).astype(jnp.bfloat16)

    att_copy = remote(att, att_other, cross_send, cross_recv, 0, x_peer)
    att_copy.start()
    bulk_send(2)
    table[...] = jnp.zeros_like(table)
    experts = router.shape[0]
    table[:experts] = router[...]
    table[LOW : LOW + experts] = router[...]
    att_copy.wait()

    wide = w_own.shape[1]
    own_cols = pl.ds(pl.multiple_of(grp * wide, wide), wide)
    other_cols = pl.ds(pl.multiple_of((1 - grp) * wide, wide), wide)
    tok = residual.shape[0]
    sums = []
    for by in (2, 1, 3, 0):
        rows_at = pl.ds(pl.multiple_of(((exp + by) % 4) * tok, tok), tok)
        piece = jnp.concatenate([att[rows_at, :], att_other[rows_at, :]], axis=0)
        partial[by] = jnp.dot(
            piece, w_own[...], preferred_element_type=jnp.float32
        ).astype(jnp.bfloat16)
        if by:
            copy = remote(
                partial.at[by], arrived.at[by - 1], sum_send, sum_recv, by - 1, at_exp(by)
            )
            copy.start()
            sums.append(copy)
    total = partial[0].astype(jnp.float32)
    for copy in sums:
        copy.wait()
    for by in range(3):
        total = total + arrived[by].astype(jnp.float32)
    crossing[...] = total[tok:].astype(jnp.bfloat16)
    cross_copy = remote(crossing, crossed, cross_send, cross_recv, 1, x_peer)
    cross_copy.start()
    bulk_send(7)
    stream[:, own_cols] = (
        residual[:, own_cols].astype(jnp.float32) + total[:tok]
    ).astype(jnp.bfloat16)
    cross_copy.wait()
    stream[:, other_cols] = (
        residual[:, other_cols].astype(jnp.float32) + crossed[...].astype(jnp.float32)
    ).astype(jnp.bfloat16)
    wide_f = stream[...].astype(jnp.float32)
    normed = (
        wide_f
        * lax.rsqrt(jnp.mean(wide_f * wide_f, axis=-1, keepdims=True) + 1e-05)
        * gain[...].reshape(1, -1)
    ).astype(jnp.bfloat16)
    width = normed.shape[1]
    logits = lax.dot_general(
        normed, table[...], (((1,), (1,)), ((), ())), preferred_element_type=jnp.float32
    )
    lane = lax.broadcasted_iota(jnp.int32, (tok, LANES), 1)
    row = lax.broadcasted_iota(jnp.int32, (LANES, tok), 0)
    expert = jnp.where(row >= LOW, row - LOW, row)
    columns = jnp.zeros((LANES, tok), jnp.float32)
    for route in range(ids.shape[0]):
        columns = columns + jnp.where(ids[route : route + 1, :] == expert, 1.0, 0.0)
    across = lax.broadcasted_iota(jnp.int32, (tok, tok), 0)
    along = lax.broadcasted_iota(jnp.int32, (tok, tok), 1)
    eye = jnp.where(across == along, 1.0, 0.0).astype(jnp.bfloat16)
    named = lax.dot_general(
        eye, columns.astype(jnp.bfloat16), (((1,), (1,)), ((), ())),
        preferred_element_type=jnp.float32,
    )
    raw = jnp.where(named > 0.0, 1.0 / (1.0 + jnp.exp(-logits)), 0.0)
    sum_raw = jnp.sum(jnp.where(lane < LOW, raw, 0.0), axis=-1, keepdims=True)
    gates = raw / sum_raw
    high = gates.astype(jnp.bfloat16)
    rest = (gates - high.astype(jnp.float32)).astype(jnp.bfloat16)
    gathered[0, :, :width] = normed
    gathered[0, :, width:] = jnp.where(
        lane < LOW, high.astype(jnp.float32), rest.astype(jnp.float32)
    ).astype(jnp.bfloat16)

    def passing(source, target, device):
        copy = remote(gathered.at[source], gathered.at[target], tok_send, tok_recv, target, device)
        copy.start()
        return copy

    first = {by: passing(0, by, at_exp(by)) for by in (2, 1, 3)}
    second, third = {}, []
    for by in (0, 1, 2, 3):
        if by:
            first[by].wait_recv()
        second[by] = passing(by, 8 + by, y_peer)
        third.append(passing(by, 4 + by, core_peer))
    for by in (0, 1, 2, 3):
        second[by].wait_recv()
        third.append(passing(8 + by, 12 + by, core_peer))
    for copy in third:
        copy.wait_recv()
    for copy in [*first.values(), *second.values(), *third]:
        copy.wait_send()
    gate_local.wait()
    down_local.wait()
    for copy in bulk:
        copy.wait()


def back_kernel(
    parts, shared, stream, out,
    one_in, one_sum, two_in, two_sum, three_in,
    one_send, one_recv, two_send, two_recv, three_send, three_recv,
):
    grp, ctx, exp = lax.axis_index("group"), lax.axis_index("ctx"), lax.axis_index("exp")
    y_peer = (grp, (ctx + 2) % 4, exp)
    core_peer = (grp, ctx + 1 - 2 * (ctx % 2), exp)

    def at_exp(by):
        return (grp, ctx, (exp + by) % 4)

    barrier = pltpu.get_barrier_semaphore()
    for peer in (y_peer, core_peer, at_exp(1), at_exp(2), at_exp(3)):
        pl.semaphore_signal(barrier, inc=1, device_id=peer, device_id_type=MESH)
    pl.semaphore_wait(barrier, 5)

    order = (2, 1, 3, 0)
    one = {}
    for far in (1, 0):
        for by in order:
            at = 4 * far + by
            one[at] = remote(
                parts.at[8 * far + 4 + by], one_in.at[at], one_send, one_recv, at, core_peer
            )
            one[at].start()
    two = {}
    for by in order:
        one[4 + by].wait_recv()
        one_sum[by] = (
            parts[8 + by].astype(jnp.float32) + one_in[4 + by].astype(jnp.float32)
        ).astype(jnp.bfloat16)
        two[by] = remote(one_sum.at[by], two_in.at[by], two_send, two_recv, by, y_peer)
        two[by].start()
    three = []
    for by in order:
        one[by].wait_recv()
        near = (
            parts[by].astype(jnp.float32)
            + one_in[by].astype(jnp.float32)
            + shared[by].astype(jnp.float32)
        )
        two[by].wait_recv()
        near = near + two_in[by].astype(jnp.float32)
        if by:
            two_sum[by - 1] = near.astype(jnp.bfloat16)
            copy = remote(
                two_sum.at[by - 1], three_in.at[by - 1], three_send, three_recv, by - 1,
                at_exp(4 - by),
            )
            copy.start()
            three.append(copy)
        else:
            total = near + stream[...].astype(jnp.float32)
    for copy in three:
        copy.wait_recv()
    for by in range(3):
        total = total + three_in[by].astype(jnp.float32)
    out[...] = total.astype(jnp.bfloat16)
    for copy in [*one.values(), *two.values(), *three]:
        copy.wait_send()


def with_kernels(
    queries, keys, values, residual_in, doc_lengths, w_out, norm_gain, router, expert_ids,
    expert_gate_up, expert_down, shared_gate_up, shared_down,
):
    bf = jnp.bfloat16
    tok, width = residual_in.shape
    heads_dev = queries.shape[1]
    rows = queries.shape[0]
    vmem, hbm = pl.BlockSpec(memory_space=pltpu.VMEM), pl.BlockSpec(memory_space=pl.ANY)
    smem = pl.BlockSpec(memory_space=pltpu.SMEM)
    dma = pltpu.SemaphoreType.DMA
    up_shape, down_shape = expert_gate_up.shape, expert_down.shape
    stream, gathered, gate_full, down_full = pl.pallas_call(
        front_kernel,
        out_shape=(
            jax.ShapeDtypeStruct((tok, width), bf),
            jax.ShapeDtypeStruct((16, tok, width + LANES), bf),
            jax.ShapeDtypeStruct((up_shape[0], 2 * up_shape[1], up_shape[2]), bf),
            jax.ShapeDtypeStruct((down_shape[0], 2 * down_shape[1], down_shape[2]), bf),
        ),
        in_specs=[smem, *[vmem] * 8, hbm, hbm],
        out_specs=(vmem, vmem, hbm, hbm),
        scratch_shapes=[
            pltpu.VMEM((3, 2, rows, HEAD), bf),
            pltpu.VMEM((rows, heads_dev), bf),
            pltpu.VMEM((rows, heads_dev), bf),
            pltpu.VMEM((4, 2 * tok, width // 2), bf),
            pltpu.VMEM((3, 2 * tok, width // 2), bf),
            pltpu.VMEM((tok, width // 2), bf),
            pltpu.VMEM((tok, width // 2), bf),
            pltpu.VMEM((LANES, width), bf),
            dma((6,)), dma((6,)), dma((3,)), dma((3,)), dma((16,)), dma((16,)),
            dma((12,)), dma((12,)), dma((2,)), dma((2,)), dma((2,)),
        ],
        compiler_params=pltpu.CompilerParams(
            collective_id=0, has_side_effects=True, vmem_limit_bytes=60 * 2**20
        ),
    )(
        doc_lengths, queries, keys, values, residual_in, w_out, norm_gain,
        router.T, expert_ids.T, expert_gate_up, expert_down,
    )
    tokens = gathered[:, :, :width].reshape(16 * tok, width)
    coded = gathered[:, :, width:].reshape(16 * tok, LANES).astype(jnp.float32)
    gates = coded[:, :LOW] + coded[:, LOW:]
    local = up_shape[0]
    first = (lax.axis_index("ctx") * lax.axis_size("exp") + lax.axis_index("exp")) * local
    hidden = down_shape[2]
    total = jnp.zeros((16 * tok, width), jnp.float32)
    for e in range(local):
        pre = jnp.dot(tokens, gate_full[e], preferred_element_type=jnp.float32)
        act = (jax.nn.silu(pre[:, :hidden]) * pre[:, hidden:]).astype(bf)
        made = lax.dot_general(
            act, down_full[e], (((1,), (1,)), ((), ())), preferred_element_type=jnp.float32
        ).astype(bf)
        is_mine = jnp.arange(LOW, dtype=jnp.int32)[None, :] == first + e
        gate = jnp.sum(jnp.where(is_mine, gates, 0.0), axis=1, keepdims=True)
        total = total + gate * made.astype(jnp.float32)
    near = tokens[: 4 * tok]
    shared_pre = jnp.einsum(
        "td,dkf->tkf", near, shared_gate_up, preferred_element_type=jnp.float32
    )
    shared_act = (jax.nn.silu(shared_pre[:, 0]) * shared_pre[:, 1]).astype(bf)
    shared = matmul(shared_act, shared_down).reshape(4, tok, width)
    return pl.pallas_call(
        back_kernel,
        out_shape=jax.ShapeDtypeStruct((tok, width), bf),
        in_specs=[vmem] * 3,
        out_specs=vmem,
        scratch_shapes=[
            pltpu.VMEM((8, tok, width), bf),
            pltpu.VMEM((4, tok, width), bf),
            pltpu.VMEM((4, tok, width), bf),
            pltpu.VMEM((3, tok, width), bf),
            pltpu.VMEM((3, tok, width), bf),
            dma((8,)), dma((8,)), dma((4,)), dma((4,)), dma((3,)), dma((3,)),
        ],
        compiler_params=pltpu.CompilerParams(
            collective_id=1, has_side_effects=True, vmem_limit_bytes=24 * 2**20
        ),
    )(total.astype(bf).reshape(16, tok, width), shared, stream)


def on_device(
    queries,
    keys,
    values,
    residual_in,
    doc_lengths,
    w_out,
    norm_gain,
    router,
    expert_ids,
    expert_gate_up,
    expert_down,
    shared_gate_up,
    shared_down,
):
    rows_dev = queries.shape[0]
    kv_count = keys.shape[1] // HEAD
    per_kv = queries.shape[1] // HEAD // kv_count
    block_count = lax.axis_size("group") * lax.axis_size("ctx")
    look_back = min(32, block_count // 2)
    my_block = lax.axis_index("group") * lax.axis_size("ctx") + lax.axis_index("ctx")
    query_pos = my_block * rows_dev + jnp.arange(rows_dev, dtype=jnp.int32)
    query_start = doc_starts(query_pos, doc_lengths)
    query_heads = queries.reshape(rows_dev, kv_count, per_kv, HEAD)
    init_state = (
        jnp.full((kv_count, per_kv, rows_dev), neg_big, jnp.float32),
        jnp.zeros((kv_count, per_kv, rows_dev), jnp.float32),
        jnp.zeros((kv_count, per_kv, rows_dev, HEAD), jnp.float32),
    )
    group_size = lax.axis_size("group")
    swap = group_size == 2
    kv_own = jnp.stack([keys, values])
    if look_back <= 8:
        blocks = [passed_along(kv_own, ("group", "ctx"), by) for by in range(look_back - 1, 0, -1)]
        kv_all = jnp.concatenate([*blocks, kv_own], axis=1)
    if swap:
        out_other, gate_other, down_other = (
            swapped(w_out), swapped(expert_gate_up), swapped(expert_down)
        )
        own_first = lax.axis_index("group") == 0
    if look_back <= 8:
        first_key = (my_block - (look_back - 1)) * rows_dev
        attended = attend_window(kv_all, first_key, query_heads, query_pos, query_start)
    else:
        soft_state = visit_block(init_state, kv_own, my_block, query_heads, query_pos, query_start)

        def cycle_turn(turn_idx, loop_state):
            moving, inner_state = loop_state
            moving = passed_along(moving, ("group", "ctx"), 1)
            return (
                moving,
                visit_block(
                    inner_state, moving, my_block - turn_idx, query_heads, query_pos, query_start
                ),
            )

        moving, soft_state = lax.fori_loop(1, look_back, cycle_turn, (kv_own, soft_state))
        run_max, run_sum, run_acc = soft_state
        attended = run_acc / run_sum[..., None]
    attended = jnp.transpose(attended, (2, 0, 1, 3)).reshape(rows_dev, -1).astype(jnp.bfloat16)
    exp_size = lax.axis_size("exp")
    exp_me = lax.axis_index("exp")
    tok_e = rows_dev // exp_size
    ahead = [(exp_me + by) % exp_size for by in range(exp_size)]
    rolled = jnp.concatenate(
        [lax.dynamic_slice_in_dim(attended, to * tok_e, tok_e, 0) for to in ahead], axis=0
    )
    if swap:
        partial = joined(own_first, matmul(rolled, w_out), matmul(rolled, out_other))
    else:
        partial = matmul(rolled, lax.all_gather(w_out, "group", axis=1, tiled=True))
    projected = summed_from(partial, exp_size, tok_e, 1)
    stream = (residual_in.astype(jnp.float32) + projected).astype(jnp.bfloat16)
    stream_f = stream.astype(jnp.float32)
    normed = (
        stream_f
        * lax.rsqrt(jnp.mean(stream_f * stream_f, axis=-1, keepdims=True) + 1e-05)
        * norm_gain
    ).astype(jnp.bfloat16)
    expert_count = router.shape[1]
    route_count = expert_ids.shape[1]
    logits = jnp.dot(normed, router, preferred_element_type=jnp.float32)
    chosen = expert_ids[:, :, None] == jnp.arange(expert_count, dtype=jnp.int32)[None, None, :]
    picked_logits = jnp.sum(jnp.where(chosen, logits[:, None, :], 0.0), axis=-1)
    raw_gates = jax.nn.sigmoid(picked_logits)
    gate_probs = raw_gates / jnp.sum(raw_gates, axis=-1, keepdims=True)
    all_normed = jnp.concatenate(
        [normed, *[turned(normed, "exp", by) for by in range(1, exp_size)]], axis=0
    )
    shared_pre = jnp.einsum(
        "td,dkf->tkf", all_normed, shared_gate_up, preferred_element_type=jnp.float32
    )
    shared_act = (jax.nn.silu(shared_pre[:, 0]) * shared_pre[:, 1]).astype(jnp.bfloat16)
    shared_out = summed_from(matmul(shared_act, shared_down), exp_size, tok_e, -1)
    slot_count = max(2, 3 * tok_e * route_count // (2 * expert_count))
    flat_ids = expert_ids.reshape(-1)
    order = jnp.arange(flat_ids.shape[0], dtype=jnp.int32)
    earlier = (flat_ids[None, :] == flat_ids[:, None]) & (order[None, :] < order[:, None])
    slot_of = jnp.sum(earlier.astype(jnp.int32), axis=1, dtype=jnp.int32)
    target = flat_ids * slot_count + slot_of
    placing = (
        jnp.arange(expert_count * slot_count, dtype=jnp.int32)[:, None] == target[None, :]
    ).astype(jnp.bfloat16)
    placing = jnp.sum(placing.reshape(expert_count * slot_count, tok_e, route_count), axis=2)
    model_width = normed.shape[1]
    outgoing = (
        jnp.dot(placing, normed, preferred_element_type=jnp.float32)
        .astype(jnp.bfloat16)
        .reshape(expert_count, slot_count, model_width)
    )
    if not swap:
        gate_up_full = lax.all_gather(expert_gate_up, "group", axis=1, tiled=True)
        down_full = lax.all_gather(expert_down, "group", axis=1, tiled=True)
    hidden_count = expert_down.shape[2]
    local_experts = expert_gate_up.shape[0]
    arrived = lax.all_to_all(outgoing, ("ctx", "exp"), split_axis=0, concat_axis=0, tiled=True)
    sources = arrived.shape[0] // local_experts
    grouped = arrived.reshape(sources, local_experts, arrived.shape[1], arrived.shape[2])
    if swap:
        half = model_width // 2
        mine = lax.dynamic_slice_in_dim(grouped, lax.axis_index("group") * half, half, 3)
        others = lax.dynamic_slice_in_dim(grouped, (1 - lax.axis_index("group")) * half, half, 3)
        pre_act = jnp.einsum(
            "nekd,edf->nekf", mine, expert_gate_up, preferred_element_type=jnp.float32
        ) + jnp.einsum("nekd,edf->nekf", others, gate_other, preferred_element_type=jnp.float32)
    else:
        pre_act = jnp.einsum(
            "nekd,edf->nekf", grouped, gate_up_full, preferred_element_type=jnp.float32
        )
    activated = (jax.nn.silu(pre_act[..., :hidden_count]) * pre_act[..., hidden_count:]).astype(
        jnp.bfloat16
    )
    def down(rows):
        return jnp.einsum(
            "nekf,edf->nekd", activated, rows, preferred_element_type=jnp.float32
        ).astype(jnp.bfloat16)

    if swap:
        result = joined(own_first, down(expert_down), down(down_other))
    else:
        result = down(down_full)
    returned = lax.all_to_all(
        result.reshape(arrived.shape), ("ctx", "exp"), split_axis=0, concat_axis=0, tiled=True
    )
    flat_back = returned.reshape(expert_count * slot_count, model_width)
    fetched = (
        jnp.take(flat_back, target, axis=0)
        .reshape(tok_e, route_count, model_width)
        .astype(jnp.float32)
    )
    routed = jnp.sum(gate_probs[:, :, None] * fetched, axis=1)
    return (stream_f + shared_out + routed).astype(jnp.bfloat16)


def solution(mesh):
    in_specs = (
        P(("group", "ctx"), "exp"),
        P(("group", "ctx"), "exp"),
        P(("group", "ctx"), "exp"),
        P(("group", "ctx", "exp"), None),
        P(),
        P("exp", "group"),
        P(),
        P(),
        P(("group", "ctx", "exp"), None),
        P(("ctx", "exp"), "group", None),
        P(("ctx", "exp"), "group", None),
        P(None, None, "exp"),
        P("exp", None),
    )
    out_specs = P(("group", "ctx", "exp"), None)
    sizes = (mesh.shape["group"], mesh.shape["ctx"], mesh.shape["exp"])
    body = with_kernels if sizes == (2, 4, 4) else on_device
    return jax.shard_map(
        body, mesh=mesh, in_specs=in_specs, out_specs=out_specs, check_vma=False
    )
```

```python
import math

import jax
import jax.numpy as jnp
from jax import lax
from jax.experimental import pallas as pl
from jax.experimental.pallas import tpu as pltpu
from jax.sharding import PartitionSpec as P

HEAD = 128


neg_big = -1e30


def passed_along(shard, axis, by):
    length = lax.axis_size(axis)
    pairs = [(i, i + by) for i in range(length) if 0 <= i + by < length]
    return lax.ppermute(shard, axis, pairs)


def doc_starts(positions, doc_lengths):
    order = jnp.arange(doc_lengths.shape[0], dtype=jnp.int32)
    before = (order[None, :] <= order[:, None]).astype(jnp.int32)
    doc_ends = jnp.sum(before * doc_lengths[None, :], axis=1, dtype=jnp.int32)
    passed = (doc_ends[None, :] <= positions[:, None]).astype(jnp.int32)
    return jnp.sum(passed * doc_lengths[None, :], axis=1, dtype=jnp.int32)


def attend_block(soft_state, kv_block, source, query_heads, query_pos, query_start):
    run_max, run_sum, run_acc = soft_state
    rows_dev = kv_block.shape[1]
    key_pos = source * rows_dev + jnp.arange(rows_dev, dtype=jnp.int32)
    allowed = (key_pos[None, :] <= query_pos[:, None]) & (key_pos[None, :] >= query_start[:, None])
    key_heads = kv_block[0].reshape(rows_dev, -1, HEAD)
    value_heads = kv_block[1].reshape(rows_dev, -1, HEAD)
    scores = jnp.einsum(
        "tgpd,sgd->gpts", query_heads, key_heads, preferred_element_type=jnp.float32
    ) * (1.0 / math.sqrt(HEAD))
    scores = jnp.where(allowed, scores, neg_big)
    new_max = jnp.maximum(run_max, jnp.max(scores, axis=-1))
    weights = jnp.where(allowed, jnp.exp(scores - new_max[..., None]), 0.0)
    factor = jnp.exp(run_max - new_max)
    run_sum = run_sum * factor + jnp.sum(weights, axis=-1)
    run_acc = run_acc * factor[..., None] + jnp.einsum(
        "gpts,sgd->gptd",
        weights.astype(jnp.bfloat16),
        value_heads,
        preferred_element_type=jnp.float32,
    )
    return (new_max, run_sum, run_acc)


def visit_block(soft_state, kv_block, source, query_heads, query_pos, query_start):
    rows_dev = kv_block.shape[1]
    useful = (source >= 0) & (source * rows_dev + rows_dev - 1 >= query_start[0])

    def run_block(inner_state):
        return attend_block(inner_state, kv_block, source, query_heads, query_pos, query_start)

    def keep_block(inner_state):
        return inner_state

    return lax.cond(useful, run_block, keep_block, soft_state)


def turned(shard, axis, by):
    length = lax.axis_size(axis)
    return lax.ppermute(shard, axis, [(i, (i + by) % length) for i in range(length)])


def swapped(shard):
    return lax.ppermute(shard, "group", [(0, 1), (1, 0)])


def matmul(rows, weights):
    return jnp.dot(rows, weights, preferred_element_type=jnp.float32).astype(jnp.bfloat16)


def joined(own_first, own, other):
    first = jnp.where(own_first, own, other)
    second = jnp.where(own_first, other, own)
    return jnp.concatenate([first, second], axis=-1)


def summed_from(partial, length, rows, step):
    total = partial[:rows].astype(jnp.float32)
    for by in range(1, length):
        piece = partial[by * rows : (by + 1) * rows]
        total = total + turned(piece, "exp", step * by).astype(jnp.float32)
    return total


def attend_window(kv, first_key, query_heads, query_pos, query_start):
    count = kv.shape[1]
    key_pos = first_key + jnp.arange(count, dtype=jnp.int32)
    allowed = (key_pos[None, :] <= query_pos[:, None]) & (key_pos[None, :] >= query_start[:, None])
    key_heads = kv[0].reshape(count, -1, HEAD)
    value_heads = kv[1].reshape(count, -1, HEAD)
    scores = jnp.einsum(
        "tgpd,sgd->gpts", query_heads, key_heads, preferred_element_type=jnp.float32
    ) * (1.0 / math.sqrt(HEAD))
    scores = jnp.where(allowed, scores, neg_big)
    weights = jnp.where(allowed, jnp.exp(scores - jnp.max(scores, axis=-1, keepdims=True)), 0.0)
    acc = jnp.einsum(
        "gpts,sgd->gptd",
        weights.astype(jnp.bfloat16),
        value_heads,
        preferred_element_type=jnp.float32,
    )
    return acc / jnp.sum(weights, axis=-1, keepdims=True)


MESH = pl.DeviceIdType.MESH
LANES = 128
LOW = 64


def remote(src, dst, sends, recvs, at, device):
    return pltpu.make_async_remote_copy(
        src_ref=src,
        dst_ref=dst,
        send_sem=sends.at[at],
        recv_sem=recvs.at[at],
        device_id=device,
        device_id_type=MESH,
    )


def front_kernel(
    lengths, q, k, v, residual, w_own, gain, router, ids, gate_up, down,
    stream, tokens, coded, gate_full, down_full,
    gathered, kv, att, att_other, partial, arrived, crossing, crossed, table,
    kv_send, kv_recv, sum_send, sum_recv, tok_send, tok_recv, big_send, big_recv, cross_send, cross_recv,
    local_sem,
):
    grp, ctx, exp = lax.axis_index("group"), lax.axis_index("ctx"), lax.axis_index("exp")
    block = grp * 4 + ctx

    def at_block(by):
        other = (block + by) % 8
        return (other // 4, other % 4, exp)

    def at_exp(by):
        return (grp, ctx, (exp + by) % 4)

    y_peer = (grp, (ctx + 2) % 4, exp)
    core_peer = (grp, ctx + 1 - 2 * (ctx % 2), exp)
    x_peer = (1 - grp, ctx, exp)
    barrier = pltpu.get_barrier_semaphore()
    for by in range(1, 8):
        pl.semaphore_signal(barrier, inc=1, device_id=at_block(by), device_id_type=MESH)
    for by in range(1, 4):
        pl.semaphore_signal(barrier, inc=1, device_id=at_exp(by), device_id_type=MESH)
    pl.semaphore_wait(barrier, 10)

    kv_copies = []
    for by in (1, 2, 3):
        for which, ref in ((0, k), (1, v)):
            copy = remote(
                ref, kv.at[by - 1, which], kv_send, kv_recv, 2 * (by - 1) + which, at_block(by)
            )
            copy.start()
            kv_copies.append(copy)
    half = gate_up.shape[1]
    piece_rows = half // 6
    bulk = []

    def bulk_send(count):
        for _ in range(count):
            at = len(bulk)
            src, full = (gate_up, gate_full) if at < 6 else (down, down_full)
            from_row = (at % 6) * piece_rows
            to_row = pl.multiple_of(grp * half + from_row, piece_rows)
            copy = remote(
                src.at[:, pl.ds(from_row, piece_rows)],
                full.at[:, pl.ds(to_row, piece_rows)],
                big_send, big_recv, at, x_peer,
            )
            copy.start()
            bulk.append(copy)

    bulk_send(2)
    mine = pl.ds(pl.multiple_of(grp * half, half), half)
    gate_local = pltpu.make_async_copy(gate_up, gate_full.at[:, mine], local_sem.at[0])
    down_local = pltpu.make_async_copy(down, down_full.at[:, mine], local_sem.at[1])
    gate_local.start()
    down_local.start()

    rows = q.shape[0]
    pos = block * rows + lax.broadcasted_iota(jnp.int32, (rows, 1), 0)
    start = jnp.zeros((rows, 1), jnp.int32)
    end = 0
    for doc in range(lengths.shape[0]):
        end = end + lengths[doc]
        start = start + jnp.where(pos >= end, lengths[doc], 0)
    key_pos = (block - 3) * rows + lax.broadcasted_iota(jnp.int32, (rows, 4 * rows), 1)
    allowed = (key_pos <= pos) & (key_pos >= start)
    for copy in kv_copies:
        copy.wait()
    keys = [kv[2, 0], kv[1, 0], kv[0, 0], k[...]]
    vals = jnp.concatenate([kv[2, 1], kv[1, 1], kv[0, 1], v[...]], axis=0)
    keys = jnp.concatenate(keys, axis=0)
    for head in range(q.shape[1] // HEAD):
        cols = pl.ds(head * HEAD, HEAD)
        scores = lax.dot_general(
            q[:, cols], keys, (((1,), (1,)), ((), ())), preferred_element_type=jnp.float32
        ) * (1.0 / math.sqrt(HEAD))
        scores = jnp.where(allowed, scores, neg_big)
        top = jnp.max(scores, axis=-1, keepdims=True)
        weights = jnp.where(allowed, jnp.exp(scores - top), 0.0)
        total = jnp.sum(weights, axis=-1, keepdims=True)
        acc = jnp.dot(
            weights.astype(jnp.bfloat16), vals, preferred_element_type=jnp.float32
        )
        att[:, cols] = (acc / total).astype(jnp.bfloat16)

    att_copy = remote(att, att_other, cross_send, cross_recv, 0, x_peer)
    att_copy.start()
    bulk_send(1)
    table[...] = jnp.zeros_like(table)
    experts = router.shape[0]
    table[:experts] = router[...]
    table[LOW : LOW + experts] = router[...]
    att_copy.wait()

    wide = w_own.shape[1]
    own_cols = pl.ds(pl.multiple_of(grp * wide, wide), wide)
    other_cols = pl.ds(pl.multiple_of((1 - grp) * wide, wide), wide)
    tok = residual.shape[0]
    sums = []
    for by in (2, 1, 3, 0):
        rows_at = pl.ds(pl.multiple_of(((exp + by) % 4) * tok, tok), tok)
        piece = jnp.concatenate([att[rows_at, :], att_other[rows_at, :]], axis=0)
        partial[by] = jnp.dot(
            piece, w_own[...], preferred_element_type=jnp.float32
        ).astype(jnp.bfloat16)
        if by:
            copy = remote(
                partial.at[by], arrived.at[by - 1], sum_send, sum_recv, by - 1, at_exp(by)
            )
            copy.start()
            sums.append(copy)
    bulk_send(1)
    total = partial[0].astype(jnp.float32)
    for copy in sums:
        copy.wait()
    for by in range(3):
        total = total + arrived[by].astype(jnp.float32)
    crossing[...] = total[tok:].astype(jnp.bfloat16)
    cross_copy = remote(crossing, crossed, cross_send, cross_recv, 1, x_peer)
    cross_copy.start()
    bulk_send(1)
    stream[:, own_cols] = (
        residual[:, own_cols].astype(jnp.float32) + total[:tok]
    ).astype(jnp.bfloat16)
    cross_copy.wait()
    stream[:, other_cols] = (
        residual[:, other_cols].astype(jnp.float32) + crossed[...].astype(jnp.float32)
    ).astype(jnp.bfloat16)
    wide_f = stream[...].astype(jnp.float32)
    normed = (
        wide_f
        * lax.rsqrt(jnp.mean(wide_f * wide_f, axis=-1, keepdims=True) + 1e-05)
        * gain[...].reshape(1, -1)
    ).astype(jnp.bfloat16)
    width = normed.shape[1]
    logits = lax.dot_general(
        normed, table[...], (((1,), (1,)), ((), ())), preferred_element_type=jnp.float32
    )
    lane = lax.broadcasted_iota(jnp.int32, (tok, LANES), 1)
    row = lax.broadcasted_iota(jnp.int32, (LANES, tok), 0)
    expert = jnp.where(row >= LOW, row - LOW, row)
    columns = jnp.zeros((LANES, tok), jnp.float32)
    for route in range(ids.shape[0]):
        columns = columns + jnp.where(ids[route : route + 1, :] == expert, 1.0, 0.0)
    across = lax.broadcasted_iota(jnp.int32, (tok, tok), 0)
    along = lax.broadcasted_iota(jnp.int32, (tok, tok), 1)
    eye = jnp.where(across == along, 1.0, 0.0).astype(jnp.bfloat16)
    named = lax.dot_general(
        eye, columns.astype(jnp.bfloat16), (((1,), (1,)), ((), ())),
        preferred_element_type=jnp.float32,
    )
    raw = jnp.where(named > 0.0, 1.0 / (1.0 + jnp.exp(-logits)), 0.0)
    sum_raw = jnp.sum(jnp.where(lane < LOW, raw, 0.0), axis=-1, keepdims=True)
    gates = raw / sum_raw
    high = gates.astype(jnp.bfloat16)
    rest = (gates - high.astype(jnp.float32)).astype(jnp.bfloat16)
    gathered[0, :, :width] = normed
    gathered[0, :, width:] = jnp.where(
        lane < LOW, high.astype(jnp.float32), rest.astype(jnp.float32)
    ).astype(jnp.bfloat16)

    def passing(source, target, device):
        copy = remote(gathered.at[source], gathered.at[target], tok_send, tok_recv, target, device)
        copy.start()
        return copy

    first = {by: passing(0, by, at_exp(by)) for by in (2, 1, 3)}
    bulk_send(1)
    second, third = {}, []
    for by in (0, 1, 2, 3):
        if by:
            first[by].wait_recv()
        second[by] = passing(by, 8 + by, y_peer)
        third.append(passing(by, 4 + by, core_peer))
        if by:
            bulk_send(1)
    for by in (0, 1, 2, 3):
        second[by].wait_recv()
        third.append(passing(8 + by, 12 + by, core_peer))
    bulk_send(3)
    for copy in third:
        copy.wait_recv()
    tokens[...] = gathered[:, :, :width]
    coded[...] = gathered[:, :, width:]
    for copy in [*first.values(), *second.values(), *third]:
        copy.wait_send()
    gate_local.wait()
    down_local.wait()
    for copy in bulk:
        copy.wait()


def back_kernel(
    parts, shared, stream, out,
    one_in, one_sum, two_in, two_sum, three_in,
    one_send, one_recv, two_send, two_recv, three_send, three_recv,
):
    grp, ctx, exp = lax.axis_index("group"), lax.axis_index("ctx"), lax.axis_index("exp")
    y_peer = (grp, (ctx + 2) % 4, exp)
    core_peer = (grp, ctx + 1 - 2 * (ctx % 2), exp)

    def at_exp(by):
        return (grp, ctx, (exp + by) % 4)

    barrier = pltpu.get_barrier_semaphore()
    for peer in (y_peer, core_peer, at_exp(1), at_exp(2), at_exp(3)):
        pl.semaphore_signal(barrier, inc=1, device_id=peer, device_id_type=MESH)
    pl.semaphore_wait(barrier, 5)

    order = (2, 1, 3, 0)
    one = {}
    for far in (1, 0):
        for by in order:
            at = 4 * far + by
            one[at] = remote(
                parts.at[8 * far + 4 + by], one_in.at[at], one_send, one_recv, at, core_peer
            )
            one[at].start()
    two = {}
    for by in order:
        one[4 + by].wait_recv()
        one_sum[by] = (
            parts[8 + by].astype(jnp.float32) + one_in[4 + by].astype(jnp.float32)
        ).astype(jnp.bfloat16)
        two[by] = remote(one_sum.at[by], two_in.at[by], two_send, two_recv, by, y_peer)
        two[by].start()
    three = []
    for by in order:
        one[by].wait_recv()
        near = (
            parts[by].astype(jnp.float32)
            + one_in[by].astype(jnp.float32)
            + shared[by].astype(jnp.float32)
        )
        two[by].wait_recv()
        near = near + two_in[by].astype(jnp.float32)
        if by:
            two_sum[by - 1] = near.astype(jnp.bfloat16)
            copy = remote(
                two_sum.at[by - 1], three_in.at[by - 1], three_send, three_recv, by - 1,
                at_exp(4 - by),
            )
            copy.start()
            three.append(copy)
        else:
            total = near + stream[...].astype(jnp.float32)
    for copy in three:
        copy.wait_recv()
    for by in range(3):
        total = total + three_in[by].astype(jnp.float32)
    out[...] = total.astype(jnp.bfloat16)
    for copy in [*one.values(), *two.values(), *three]:
        copy.wait_send()


def with_kernels(
    queries, keys, values, residual_in, doc_lengths, w_out, norm_gain, router, expert_ids,
    expert_gate_up, expert_down, shared_gate_up, shared_down,
):
    bf = jnp.bfloat16
    tok, width = residual_in.shape
    heads_dev = queries.shape[1]
    rows = queries.shape[0]
    vmem, hbm = pl.BlockSpec(memory_space=pltpu.VMEM), pl.BlockSpec(memory_space=pl.ANY)
    smem = pl.BlockSpec(memory_space=pltpu.SMEM)
    dma = pltpu.SemaphoreType.DMA
    up_shape, down_shape = expert_gate_up.shape, expert_down.shape
    stream, tokens, coded, gate_full, down_full = pl.pallas_call(
        front_kernel,
        out_shape=(
            jax.ShapeDtypeStruct((tok, width), bf),
            jax.ShapeDtypeStruct((16, tok, width), bf),
            jax.ShapeDtypeStruct((16, tok, LANES), bf),
            jax.ShapeDtypeStruct((up_shape[0], 2 * up_shape[1], up_shape[2]), bf),
            jax.ShapeDtypeStruct((down_shape[0], 2 * down_shape[1], down_shape[2]), bf),
        ),
        in_specs=[smem, *[vmem] * 8, hbm, hbm],
        out_specs=(vmem, vmem, vmem, hbm, hbm),
        scratch_shapes=[
            pltpu.VMEM((16, tok, width + LANES), bf),
            pltpu.VMEM((3, 2, rows, HEAD), bf),
            pltpu.VMEM((rows, heads_dev), bf),
            pltpu.VMEM((rows, heads_dev), bf),
            pltpu.VMEM((4, 2 * tok, width // 2), bf),
            pltpu.VMEM((3, 2 * tok, width // 2), bf),
            pltpu.VMEM((tok, width // 2), bf),
            pltpu.VMEM((tok, width // 2), bf),
            pltpu.VMEM((LANES, width), bf),
            dma((6,)), dma((6,)), dma((3,)), dma((3,)), dma((16,)), dma((16,)),
            dma((12,)), dma((12,)), dma((2,)), dma((2,)), dma((2,)),
        ],
        compiler_params=pltpu.CompilerParams(
            collective_id=0, has_side_effects=True, vmem_limit_bytes=60 * 2**20
        ),
    )(
        doc_lengths, queries, keys, values, residual_in, w_out, norm_gain,
        router.T, expert_ids.T, expert_gate_up, expert_down,
    )
    tokens = tokens.reshape(16 * tok, width)
    coded = coded.reshape(16 * tok, LANES).astype(jnp.float32)
    gates = coded[:, :LOW] + coded[:, LOW:]
    local = up_shape[0]
    first = (lax.axis_index("ctx") * lax.axis_size("exp") + lax.axis_index("exp")) * local
    hidden = down_shape[2]
    total = jnp.zeros((16 * tok, width), jnp.float32)
    for e in range(local):
        pre = jnp.dot(tokens, gate_full[e], preferred_element_type=jnp.float32)
        act = (jax.nn.silu(pre[:, :hidden]) * pre[:, hidden:]).astype(bf)
        made = lax.dot_general(
            act, down_full[e], (((1,), (1,)), ((), ())), preferred_element_type=jnp.float32
        ).astype(bf)
        is_mine = jnp.arange(LOW, dtype=jnp.int32)[None, :] == first + e
        gate = jnp.sum(jnp.where(is_mine, gates, 0.0), axis=1, keepdims=True)
        total = total + gate * made.astype(jnp.float32)
    near = tokens[: 4 * tok]
    shared_pre = jnp.einsum(
        "td,dkf->tkf", near, shared_gate_up, preferred_element_type=jnp.float32
    )
    shared_act = (jax.nn.silu(shared_pre[:, 0]) * shared_pre[:, 1]).astype(bf)
    shared = matmul(shared_act, shared_down).reshape(4, tok, width)
    return pl.pallas_call(
        back_kernel,
        out_shape=jax.ShapeDtypeStruct((tok, width), bf),
        in_specs=[vmem] * 3,
        out_specs=vmem,
        scratch_shapes=[
            pltpu.VMEM((8, tok, width), bf),
            pltpu.VMEM((4, tok, width), bf),
            pltpu.VMEM((4, tok, width), bf),
            pltpu.VMEM((3, tok, width), bf),
            pltpu.VMEM((3, tok, width), bf),
            dma((8,)), dma((8,)), dma((4,)), dma((4,)), dma((3,)), dma((3,)),
        ],
        compiler_params=pltpu.CompilerParams(
            collective_id=1, has_side_effects=True, vmem_limit_bytes=24 * 2**20
        ),
    )(total.astype(bf).reshape(16, tok, width), shared, stream)


def on_device(
    queries,
    keys,
    values,
    residual_in,
    doc_lengths,
    w_out,
    norm_gain,
    router,
    expert_ids,
    expert_gate_up,
    expert_down,
    shared_gate_up,
    shared_down,
):
    rows_dev = queries.shape[0]
    kv_count = keys.shape[1] // HEAD
    per_kv = queries.shape[1] // HEAD // kv_count
    block_count = lax.axis_size("group") * lax.axis_size("ctx")
    look_back = min(32, block_count // 2)
    my_block = lax.axis_index("group") * lax.axis_size("ctx") + lax.axis_index("ctx")
    query_pos = my_block * rows_dev + jnp.arange(rows_dev, dtype=jnp.int32)
    query_start = doc_starts(query_pos, doc_lengths)
    query_heads = queries.reshape(rows_dev, kv_count, per_kv, HEAD)
    init_state = (
        jnp.full((kv_count, per_kv, rows_dev), neg_big, jnp.float32),
        jnp.zeros((kv_count, per_kv, rows_dev), jnp.float32),
        jnp.zeros((kv_count, per_kv, rows_dev, HEAD), jnp.float32),
    )
    group_size = lax.axis_size("group")
    swap = group_size == 2
    kv_own = jnp.stack([keys, values])
    if look_back <= 8:
        blocks = [passed_along(kv_own, ("group", "ctx"), by) for by in range(look_back - 1, 0, -1)]
        kv_all = jnp.concatenate([*blocks, kv_own], axis=1)
    if swap:
        out_other, gate_other, down_other = (
            swapped(w_out), swapped(expert_gate_up), swapped(expert_down)
        )
        own_first = lax.axis_index("group") == 0
    if look_back <= 8:
        first_key = (my_block - (look_back - 1)) * rows_dev
        attended = attend_window(kv_all, first_key, query_heads, query_pos, query_start)
    else:
        soft_state = visit_block(init_state, kv_own, my_block, query_heads, query_pos, query_start)

        def cycle_turn(turn_idx, loop_state):
            moving, inner_state = loop_state
            moving = passed_along(moving, ("group", "ctx"), 1)
            return (
                moving,
                visit_block(
                    inner_state, moving, my_block - turn_idx, query_heads, query_pos, query_start
                ),
            )

        moving, soft_state = lax.fori_loop(1, look_back, cycle_turn, (kv_own, soft_state))
        run_max, run_sum, run_acc = soft_state
        attended = run_acc / run_sum[..., None]
    attended = jnp.transpose(attended, (2, 0, 1, 3)).reshape(rows_dev, -1).astype(jnp.bfloat16)
    exp_size = lax.axis_size("exp")
    exp_me = lax.axis_index("exp")
    tok_e = rows_dev // exp_size
    ahead = [(exp_me + by) % exp_size for by in range(exp_size)]
    rolled = jnp.concatenate(
        [lax.dynamic_slice_in_dim(attended, to * tok_e, tok_e, 0) for to in ahead], axis=0
    )
    if swap:
        partial = joined(own_first, matmul(rolled, w_out), matmul(rolled, out_other))
    else:
        partial = matmul(rolled, lax.all_gather(w_out, "group", axis=1, tiled=True))
    projected = summed_from(partial, exp_size, tok_e, 1)
    stream = (residual_in.astype(jnp.float32) + projected).astype(jnp.bfloat16)
    stream_f = stream.astype(jnp.float32)
    normed = (
        stream_f
        * lax.rsqrt(jnp.mean(stream_f * stream_f, axis=-1, keepdims=True) + 1e-05)
        * norm_gain
    ).astype(jnp.bfloat16)
    expert_count = router.shape[1]
    route_count = expert_ids.shape[1]
    logits = jnp.dot(normed, router, preferred_element_type=jnp.float32)
    chosen = expert_ids[:, :, None] == jnp.arange(expert_count, dtype=jnp.int32)[None, None, :]
    picked_logits = jnp.sum(jnp.where(chosen, logits[:, None, :], 0.0), axis=-1)
    raw_gates = jax.nn.sigmoid(picked_logits)
    gate_probs = raw_gates / jnp.sum(raw_gates, axis=-1, keepdims=True)
    all_normed = jnp.concatenate(
        [normed, *[turned(normed, "exp", by) for by in range(1, exp_size)]], axis=0
    )
    shared_pre = jnp.einsum(
        "td,dkf->tkf", all_normed, shared_gate_up, preferred_element_type=jnp.float32
    )
    shared_act = (jax.nn.silu(shared_pre[:, 0]) * shared_pre[:, 1]).astype(jnp.bfloat16)
    shared_out = summed_from(matmul(shared_act, shared_down), exp_size, tok_e, -1)
    slot_count = max(2, 3 * tok_e * route_count // (2 * expert_count))
    flat_ids = expert_ids.reshape(-1)
    order = jnp.arange(flat_ids.shape[0], dtype=jnp.int32)
    earlier = (flat_ids[None, :] == flat_ids[:, None]) & (order[None, :] < order[:, None])
    slot_of = jnp.sum(earlier.astype(jnp.int32), axis=1, dtype=jnp.int32)
    target = flat_ids * slot_count + slot_of
    placing = (
        jnp.arange(expert_count * slot_count, dtype=jnp.int32)[:, None] == target[None, :]
    ).astype(jnp.bfloat16)
    placing = jnp.sum(placing.reshape(expert_count * slot_count, tok_e, route_count), axis=2)
    model_width = normed.shape[1]
    outgoing = (
        jnp.dot(placing, normed, preferred_element_type=jnp.float32)
        .astype(jnp.bfloat16)
        .reshape(expert_count, slot_count, model_width)
    )
    if not swap:
        gate_up_full = lax.all_gather(expert_gate_up, "group", axis=1, tiled=True)
        down_full = lax.all_gather(expert_down, "group", axis=1, tiled=True)
    hidden_count = expert_down.shape[2]
    local_experts = expert_gate_up.shape[0]
    arrived = lax.all_to_all(outgoing, ("ctx", "exp"), split_axis=0, concat_axis=0, tiled=True)
    sources = arrived.shape[0] // local_experts
    grouped = arrived.reshape(sources, local_experts, arrived.shape[1], arrived.shape[2])
    if swap:
        half = model_width // 2
        mine = lax.dynamic_slice_in_dim(grouped, lax.axis_index("group") * half, half, 3)
        others = lax.dynamic_slice_in_dim(grouped, (1 - lax.axis_index("group")) * half, half, 3)
        pre_act = jnp.einsum(
            "nekd,edf->nekf", mine, expert_gate_up, preferred_element_type=jnp.float32
        ) + jnp.einsum("nekd,edf->nekf", others, gate_other, preferred_element_type=jnp.float32)
    else:
        pre_act = jnp.einsum(
            "nekd,edf->nekf", grouped, gate_up_full, preferred_element_type=jnp.float32
        )
    activated = (jax.nn.silu(pre_act[..., :hidden_count]) * pre_act[..., hidden_count:]).astype(
        jnp.bfloat16
    )
    def down(rows):
        return jnp.einsum(
            "nekf,edf->nekd", activated, rows, preferred_element_type=jnp.float32
        ).astype(jnp.bfloat16)

    if swap:
        result = joined(own_first, down(expert_down), down(down_other))
    else:
        result = down(down_full)
    returned = lax.all_to_all(
        result.reshape(arrived.shape), ("ctx", "exp"), split_axis=0, concat_axis=0, tiled=True
    )
    flat_back = returned.reshape(expert_count * slot_count, model_width)
    fetched = (
        jnp.take(flat_back, target, axis=0)
        .reshape(tok_e, route_count, model_width)
        .astype(jnp.float32)
    )
    routed = jnp.sum(gate_probs[:, :, None] * fetched, axis=1)
    return (stream_f + shared_out + routed).astype(jnp.bfloat16)


def solution(mesh):
    in_specs = (
        P(("group", "ctx"), "exp"),
        P(("group", "ctx"), "exp"),
        P(("group", "ctx"), "exp"),
        P(("group", "ctx", "exp"), None),
        P(),
        P("exp", "group"),
        P(),
        P(),
        P(("group", "ctx", "exp"), None),
        P(("ctx", "exp"), "group", None),
        P(("ctx", "exp"), "group", None),
        P(None, None, "exp"),
        P("exp", None),
    )
    out_specs = P(("group", "ctx", "exp"), None)
    sizes = (mesh.shape["group"], mesh.shape["ctx"], mesh.shape["exp"])
    body = with_kernels if sizes == (2, 4, 4) else on_device
    return jax.shard_map(
        body, mesh=mesh, in_specs=in_specs, out_specs=out_specs, check_vma=False
    )
```

```python
import math

import jax
import jax.numpy as jnp
from jax import lax
from jax.experimental import pallas as pl
from jax.experimental.pallas import tpu as pltpu
from jax.sharding import PartitionSpec as P

HEAD = 128


neg_big = -1e30


def passed_along(shard, axis, by):
    length = lax.axis_size(axis)
    pairs = [(i, i + by) for i in range(length) if 0 <= i + by < length]
    return lax.ppermute(shard, axis, pairs)


def doc_starts(positions, doc_lengths):
    order = jnp.arange(doc_lengths.shape[0], dtype=jnp.int32)
    before = (order[None, :] <= order[:, None]).astype(jnp.int32)
    doc_ends = jnp.sum(before * doc_lengths[None, :], axis=1, dtype=jnp.int32)
    passed = (doc_ends[None, :] <= positions[:, None]).astype(jnp.int32)
    return jnp.sum(passed * doc_lengths[None, :], axis=1, dtype=jnp.int32)


def attend_block(soft_state, kv_block, source, query_heads, query_pos, query_start):
    run_max, run_sum, run_acc = soft_state
    rows_dev = kv_block.shape[1]
    key_pos = source * rows_dev + jnp.arange(rows_dev, dtype=jnp.int32)
    allowed = (key_pos[None, :] <= query_pos[:, None]) & (key_pos[None, :] >= query_start[:, None])
    key_heads = kv_block[0].reshape(rows_dev, -1, HEAD)
    value_heads = kv_block[1].reshape(rows_dev, -1, HEAD)
    scores = jnp.einsum(
        "tgpd,sgd->gpts", query_heads, key_heads, preferred_element_type=jnp.float32
    ) * (1.0 / math.sqrt(HEAD))
    scores = jnp.where(allowed, scores, neg_big)
    new_max = jnp.maximum(run_max, jnp.max(scores, axis=-1))
    weights = jnp.where(allowed, jnp.exp(scores - new_max[..., None]), 0.0)
    factor = jnp.exp(run_max - new_max)
    run_sum = run_sum * factor + jnp.sum(weights, axis=-1)
    run_acc = run_acc * factor[..., None] + jnp.einsum(
        "gpts,sgd->gptd",
        weights.astype(jnp.bfloat16),
        value_heads,
        preferred_element_type=jnp.float32,
    )
    return (new_max, run_sum, run_acc)


def visit_block(soft_state, kv_block, source, query_heads, query_pos, query_start):
    rows_dev = kv_block.shape[1]
    useful = (source >= 0) & (source * rows_dev + rows_dev - 1 >= query_start[0])

    def run_block(inner_state):
        return attend_block(inner_state, kv_block, source, query_heads, query_pos, query_start)

    def keep_block(inner_state):
        return inner_state

    return lax.cond(useful, run_block, keep_block, soft_state)


def turned(shard, axis, by):
    length = lax.axis_size(axis)
    return lax.ppermute(shard, axis, [(i, (i + by) % length) for i in range(length)])


def swapped(shard):
    return lax.ppermute(shard, "group", [(0, 1), (1, 0)])


def matmul(rows, weights):
    return jnp.dot(rows, weights, preferred_element_type=jnp.float32).astype(jnp.bfloat16)


def joined(own_first, own, other):
    first = jnp.where(own_first, own, other)
    second = jnp.where(own_first, other, own)
    return jnp.concatenate([first, second], axis=-1)


def summed_from(partial, length, rows, step):
    total = partial[:rows].astype(jnp.float32)
    for by in range(1, length):
        piece = partial[by * rows : (by + 1) * rows]
        total = total + turned(piece, "exp", step * by).astype(jnp.float32)
    return total


def attend_window(kv, first_key, query_heads, query_pos, query_start):
    count = kv.shape[1]
    key_pos = first_key + jnp.arange(count, dtype=jnp.int32)
    allowed = (key_pos[None, :] <= query_pos[:, None]) & (key_pos[None, :] >= query_start[:, None])
    key_heads = kv[0].reshape(count, -1, HEAD)
    value_heads = kv[1].reshape(count, -1, HEAD)
    scores = jnp.einsum(
        "tgpd,sgd->gpts", query_heads, key_heads, preferred_element_type=jnp.float32
    ) * (1.0 / math.sqrt(HEAD))
    scores = jnp.where(allowed, scores, neg_big)
    weights = jnp.where(allowed, jnp.exp(scores - jnp.max(scores, axis=-1, keepdims=True)), 0.0)
    acc = jnp.einsum(
        "gpts,sgd->gptd",
        weights.astype(jnp.bfloat16),
        value_heads,
        preferred_element_type=jnp.float32,
    )
    return acc / jnp.sum(weights, axis=-1, keepdims=True)


MESH = pl.DeviceIdType.MESH
LANES = 128
LOW = 64


def remote(src, dst, sends, recvs, at, device):
    return pltpu.make_async_remote_copy(
        src_ref=src,
        dst_ref=dst,
        send_sem=sends.at[at],
        recv_sem=recvs.at[at],
        device_id=device,
        device_id_type=MESH,
    )


def front_kernel(
    lengths, q, k, v, residual, w_own, gain, router, ids, gate_up, down,
    stream, tokens, coded, gate_full, down_full,
    gathered, kv, att, att_other, partial, arrived, crossing, crossed, table,
    kv_send, kv_recv, sum_send, sum_recv, tok_send, tok_recv, big_send, big_recv, cross_send, cross_recv,
    local_sem,
):
    grp, ctx, exp = lax.axis_index("group"), lax.axis_index("ctx"), lax.axis_index("exp")
    block = grp * 4 + ctx

    def at_block(by):
        other = (block + by) % 8
        return (other // 4, other % 4, exp)

    def at_exp(by):
        return (grp, ctx, (exp + by) % 4)

    y_peer = (grp, (ctx + 2) % 4, exp)
    core_peer = (grp, ctx + 1 - 2 * (ctx % 2), exp)
    x_peer = (1 - grp, ctx, exp)
    barrier = pltpu.get_barrier_semaphore()
    for by in range(1, 8):
        pl.semaphore_signal(barrier, inc=1, device_id=at_block(by), device_id_type=MESH)
    for by in range(1, 4):
        pl.semaphore_signal(barrier, inc=1, device_id=at_exp(by), device_id_type=MESH)
    pl.semaphore_wait(barrier, 10)

    kv_copies = []
    for by in (1, 2, 3):
        for which, ref in ((0, k), (1, v)):
            copy = remote(
                ref, kv.at[by - 1, which], kv_send, kv_recv, 2 * (by - 1) + which, at_block(by)
            )
            copy.start()
            kv_copies.append(copy)
    half = gate_up.shape[1]
    piece_rows = half // 6
    bulk = []

    def bulk_send(count):
        for _ in range(count):
            at = len(bulk)
            src, full = (gate_up, gate_full) if at < 6 else (down, down_full)
            from_row = (at % 6) * piece_rows
            to_row = pl.multiple_of(grp * half + from_row, piece_rows)
            copy = remote(
                src.at[:, pl.ds(from_row, piece_rows)],
                full.at[:, pl.ds(to_row, piece_rows)],
                big_send, big_recv, at, x_peer,
            )
            copy.start()
            bulk.append(copy)

    bulk_send(2)
    mine = pl.ds(pl.multiple_of(grp * half, half), half)
    gate_local = pltpu.make_async_copy(gate_up, gate_full.at[:, mine], local_sem.at[0])
    down_local = pltpu.make_async_copy(down, down_full.at[:, mine], local_sem.at[1])
    gate_local.start()
    down_local.start()

    rows = q.shape[0]
    pos = block * rows + lax.broadcasted_iota(jnp.int32, (rows, 1), 0)
    start = jnp.zeros((rows, 1), jnp.int32)
    end = 0
    for doc in range(lengths.shape[0]):
        end = end + lengths[doc]
        start = start + jnp.where(pos >= end, lengths[doc], 0)
    key_pos = (block - 3) * rows + lax.broadcasted_iota(jnp.int32, (rows, 4 * rows), 1)
    allowed = (key_pos <= pos) & (key_pos >= start)
    for copy in kv_copies:
        copy.wait()
    keys = [kv[2, 0], kv[1, 0], kv[0, 0], k[...]]
    vals = jnp.concatenate([kv[2, 1], kv[1, 1], kv[0, 1], v[...]], axis=0)
    keys = jnp.concatenate(keys, axis=0)
    for head in range(q.shape[1] // HEAD):
        cols = pl.ds(head * HEAD, HEAD)
        scores = lax.dot_general(
            q[:, cols], keys, (((1,), (1,)), ((), ())), preferred_element_type=jnp.float32
        ) * (1.0 / math.sqrt(HEAD))
        scores = jnp.where(allowed, scores, neg_big)
        top = jnp.max(scores, axis=-1, keepdims=True)
        weights = jnp.where(allowed, jnp.exp(scores - top), 0.0)
        total = jnp.sum(weights, axis=-1, keepdims=True)
        acc = jnp.dot(
            weights.astype(jnp.bfloat16), vals, preferred_element_type=jnp.float32
        )
        att[:, cols] = (acc / total).astype(jnp.bfloat16)

    att_copy = remote(att, att_other, cross_send, cross_recv, 0, x_peer)
    att_copy.start()
    bulk_send(1)
    table[...] = jnp.zeros_like(table)
    experts = router.shape[0]
    table[:experts] = router[...]
    table[LOW : LOW + experts] = router[...]
    att_copy.wait()

    wide = w_own.shape[1]
    own_cols = pl.ds(pl.multiple_of(grp * wide, wide), wide)
    other_cols = pl.ds(pl.multiple_of((1 - grp) * wide, wide), wide)
    tok = residual.shape[0]
    sums = []
    for by in (2, 1, 3, 0):
        rows_at = pl.ds(pl.multiple_of(((exp + by) % 4) * tok, tok), tok)
        piece = jnp.concatenate([att[rows_at, :], att_other[rows_at, :]], axis=0)
        partial[by] = jnp.dot(
            piece, w_own[...], preferred_element_type=jnp.float32
        ).astype(jnp.bfloat16)
        if by:
            copy = remote(
                partial.at[by], arrived.at[by - 1], sum_send, sum_recv, by - 1, at_exp(by)
            )
            copy.start()
            sums.append(copy)
    bulk_send(1)
    total = partial[0].astype(jnp.float32)
    for copy in sums:
        copy.wait()
    for by in range(3):
        total = total + arrived[by].astype(jnp.float32)
    crossing[...] = total[tok:].astype(jnp.bfloat16)
    cross_copy = remote(crossing, crossed, cross_send, cross_recv, 1, x_peer)
    cross_copy.start()
    bulk_send(1)
    stream[:, own_cols] = (
        residual[:, own_cols].astype(jnp.float32) + total[:tok]
    ).astype(jnp.bfloat16)
    cross_copy.wait()
    stream[:, other_cols] = (
        residual[:, other_cols].astype(jnp.float32) + crossed[...].astype(jnp.float32)
    ).astype(jnp.bfloat16)
    wide_f = stream[...].astype(jnp.float32)
    normed = (
        wide_f
        * lax.rsqrt(jnp.mean(wide_f * wide_f, axis=-1, keepdims=True) + 1e-05)
        * gain[...].reshape(1, -1)
    ).astype(jnp.bfloat16)
    width = normed.shape[1]
    logits = lax.dot_general(
        normed, table[...], (((1,), (1,)), ((), ())), preferred_element_type=jnp.float32
    )
    lane = lax.broadcasted_iota(jnp.int32, (tok, LANES), 1)
    row = lax.broadcasted_iota(jnp.int32, (LANES, tok), 0)
    expert = jnp.where(row >= LOW, row - LOW, row)
    columns = jnp.zeros((LANES, tok), jnp.float32)
    for route in range(ids.shape[0]):
        columns = columns + jnp.where(ids[route : route + 1, :] == expert, 1.0, 0.0)
    across = lax.broadcasted_iota(jnp.int32, (tok, tok), 0)
    along = lax.broadcasted_iota(jnp.int32, (tok, tok), 1)
    eye = jnp.where(across == along, 1.0, 0.0).astype(jnp.bfloat16)
    named = lax.dot_general(
        eye, columns.astype(jnp.bfloat16), (((1,), (1,)), ((), ())),
        preferred_element_type=jnp.float32,
    )
    raw = jnp.where(named > 0.0, 1.0 / (1.0 + jnp.exp(-logits)), 0.0)
    sum_raw = jnp.sum(jnp.where(lane < LOW, raw, 0.0), axis=-1, keepdims=True)
    gates = raw / sum_raw
    high = gates.astype(jnp.bfloat16)
    rest = (gates - high.astype(jnp.float32)).astype(jnp.bfloat16)
    gathered[0, :, :width] = normed
    gathered[0, :, width:] = jnp.where(
        lane < LOW, high.astype(jnp.float32), rest.astype(jnp.float32)
    ).astype(jnp.bfloat16)

    def passing(source, target, device):
        copy = remote(gathered.at[source], gathered.at[target], tok_send, tok_recv, target, device)
        copy.start()
        return copy

    first = {by: passing(0, by, at_exp(by)) for by in (2, 1, 3)}
    bulk_send(1)
    second, third = {}, []
    for by in (0, 1, 2, 3):
        if by:
            first[by].wait_recv()
        second[by] = passing(by, 8 + by, y_peer)
        third.append(passing(by, 4 + by, core_peer))
        if by:
            bulk_send(1)
    for by in (0, 1, 2, 3):
        second[by].wait_recv()
        third.append(passing(8 + by, 12 + by, core_peer))
    bulk_send(3)
    for copy in third:
        copy.wait_recv()
    tokens[...] = gathered[:, :, :width]
    coded[...] = gathered[:, :, width:]
    for copy in [*first.values(), *second.values(), *third]:
        copy.wait_send()
    gate_local.wait()
    down_local.wait()
    for copy in bulk:
        copy.wait()


def back_kernel(
    parts, shared, stream, out,
    one_in, one_sum, two_in, two_sum, three_in,
    one_send, one_recv, two_send, two_recv, three_send, three_recv,
):
    grp, ctx, exp = lax.axis_index("group"), lax.axis_index("ctx"), lax.axis_index("exp")
    y_peer = (grp, (ctx + 2) % 4, exp)
    core_peer = (grp, ctx + 1 - 2 * (ctx % 2), exp)

    def at_exp(by):
        return (grp, ctx, (exp + by) % 4)

    barrier = pltpu.get_barrier_semaphore()
    for peer in (y_peer, core_peer, at_exp(1), at_exp(2), at_exp(3)):
        pl.semaphore_signal(barrier, inc=1, device_id=peer, device_id_type=MESH)
    pl.semaphore_wait(barrier, 5)

    order = (2, 1, 3, 0)
    one = {}
    for far in (1, 0):
        for by in order:
            at = 4 * far + by
            one[at] = remote(
                parts.at[8 * far + 4 + by], one_in.at[at], one_send, one_recv, at, core_peer
            )
            one[at].start()
    two = {}
    for by in order:
        one[4 + by].wait_recv()
        one_sum[by] = (
            parts[8 + by].astype(jnp.float32) + one_in[4 + by].astype(jnp.float32)
        ).astype(jnp.bfloat16)
        two[by] = remote(one_sum.at[by], two_in.at[by], two_send, two_recv, by, y_peer)
        two[by].start()
    three = []
    for by in order:
        one[by].wait_recv()
        near = (
            parts[by].astype(jnp.float32)
            + one_in[by].astype(jnp.float32)
            + shared[by].astype(jnp.float32)
        )
        two[by].wait_recv()
        near = near + two_in[by].astype(jnp.float32)
        if by:
            two_sum[by - 1] = near.astype(jnp.bfloat16)
            copy = remote(
                two_sum.at[by - 1], three_in.at[by - 1], three_send, three_recv, by - 1,
                at_exp(4 - by),
            )
            copy.start()
            three.append(copy)
        else:
            total = near + stream[...].astype(jnp.float32)
    for copy in three:
        copy.wait_recv()
    for by in range(3):
        total = total + three_in[by].astype(jnp.float32)
    out[...] = total.astype(jnp.bfloat16)
    for copy in [*one.values(), *two.values(), *three]:
        copy.wait_send()


def with_kernels(
    queries, keys, values, residual_in, doc_lengths, w_out, norm_gain, router, expert_ids,
    expert_gate_up, expert_down, shared_gate_up, shared_down,
):
    bf = jnp.bfloat16
    tok, width = residual_in.shape
    heads_dev = queries.shape[1]
    rows = queries.shape[0]
    vmem, hbm = pl.BlockSpec(memory_space=pltpu.VMEM), pl.BlockSpec(memory_space=pl.ANY)
    smem = pl.BlockSpec(memory_space=pltpu.SMEM)
    dma = pltpu.SemaphoreType.DMA
    up_shape, down_shape = expert_gate_up.shape, expert_down.shape
    stream, tokens, coded, gate_full, down_full = pl.pallas_call(
        front_kernel,
        out_shape=(
            jax.ShapeDtypeStruct((tok, width), bf),
            jax.ShapeDtypeStruct((16, tok, width), bf),
            jax.ShapeDtypeStruct((16, tok, LANES), bf),
            jax.ShapeDtypeStruct((up_shape[0], 2 * up_shape[1], up_shape[2]), bf),
            jax.ShapeDtypeStruct((down_shape[0], 2 * down_shape[1], down_shape[2]), bf),
        ),
        in_specs=[smem, *[vmem] * 8, hbm, hbm],
        out_specs=(vmem, vmem, vmem, hbm, hbm),
        scratch_shapes=[
            pltpu.VMEM((16, tok, width + LANES), bf),
            pltpu.VMEM((3, 2, rows, HEAD), bf),
            pltpu.VMEM((rows, heads_dev), bf),
            pltpu.VMEM((rows, heads_dev), bf),
            pltpu.VMEM((4, 2 * tok, width // 2), bf),
            pltpu.VMEM((3, 2 * tok, width // 2), bf),
            pltpu.VMEM((tok, width // 2), bf),
            pltpu.VMEM((tok, width // 2), bf),
            pltpu.VMEM((LANES, width), bf),
            dma((6,)), dma((6,)), dma((3,)), dma((3,)), dma((16,)), dma((16,)),
            dma((12,)), dma((12,)), dma((2,)), dma((2,)), dma((2,)),
        ],
        compiler_params=pltpu.CompilerParams(
            collective_id=0, has_side_effects=True, vmem_limit_bytes=24 * 2**20
        ),
    )(
        doc_lengths, queries, keys, values, residual_in, w_out, norm_gain,
        router.T, expert_ids.T, expert_gate_up, expert_down,
    )
    tokens = tokens.reshape(16 * tok, width)
    coded = coded.reshape(16 * tok, LANES).astype(jnp.float32)
    gates = coded[:, :LOW] + coded[:, LOW:]
    local = up_shape[0]
    first = (lax.axis_index("ctx") * lax.axis_size("exp") + lax.axis_index("exp")) * local
    hidden = down_shape[2]
    total = jnp.zeros((16 * tok, width), jnp.float32)
    for e in range(local):
        pre = jnp.dot(tokens, gate_full[e], preferred_element_type=jnp.float32)
        act = (jax.nn.silu(pre[:, :hidden]) * pre[:, hidden:]).astype(bf)
        made = lax.dot_general(
            act, down_full[e], (((1,), (1,)), ((), ())), preferred_element_type=jnp.float32
        ).astype(bf)
        is_mine = jnp.arange(LOW, dtype=jnp.int32)[None, :] == first + e
        gate = jnp.sum(jnp.where(is_mine, gates, 0.0), axis=1, keepdims=True)
        total = total + gate * made.astype(jnp.float32)
    near = tokens[: 4 * tok]
    shared_pre = jnp.einsum(
        "td,dkf->tkf", near, shared_gate_up, preferred_element_type=jnp.float32
    )
    shared_act = (jax.nn.silu(shared_pre[:, 0]) * shared_pre[:, 1]).astype(bf)
    shared = matmul(shared_act, shared_down).reshape(4, tok, width)
    return pl.pallas_call(
        back_kernel,
        out_shape=jax.ShapeDtypeStruct((tok, width), bf),
        in_specs=[vmem] * 3,
        out_specs=vmem,
        scratch_shapes=[
            pltpu.VMEM((8, tok, width), bf),
            pltpu.VMEM((4, tok, width), bf),
            pltpu.VMEM((4, tok, width), bf),
            pltpu.VMEM((3, tok, width), bf),
            pltpu.VMEM((3, tok, width), bf),
            dma((8,)), dma((8,)), dma((4,)), dma((4,)), dma((3,)), dma((3,)),
        ],
        compiler_params=pltpu.CompilerParams(
            collective_id=1, has_side_effects=True, vmem_limit_bytes=24 * 2**20
        ),
    )(total.astype(bf).reshape(16, tok, width), shared, stream)


def on_device(
    queries,
    keys,
    values,
    residual_in,
    doc_lengths,
    w_out,
    norm_gain,
    router,
    expert_ids,
    expert_gate_up,
    expert_down,
    shared_gate_up,
    shared_down,
):
    rows_dev = queries.shape[0]
    kv_count = keys.shape[1] // HEAD
    per_kv = queries.shape[1] // HEAD // kv_count
    block_count = lax.axis_size("group") * lax.axis_size("ctx")
    look_back = min(32, block_count // 2)
    my_block = lax.axis_index("group") * lax.axis_size("ctx") + lax.axis_index("ctx")
    query_pos = my_block * rows_dev + jnp.arange(rows_dev, dtype=jnp.int32)
    query_start = doc_starts(query_pos, doc_lengths)
    query_heads = queries.reshape(rows_dev, kv_count, per_kv, HEAD)
    init_state = (
        jnp.full((kv_count, per_kv, rows_dev), neg_big, jnp.float32),
        jnp.zeros((kv_count, per_kv, rows_dev), jnp.float32),
        jnp.zeros((kv_count, per_kv, rows_dev, HEAD), jnp.float32),
    )
    group_size = lax.axis_size("group")
    swap = group_size == 2
    kv_own = jnp.stack([keys, values])
    if look_back <= 8:
        blocks = [passed_along(kv_own, ("group", "ctx"), by) for by in range(look_back - 1, 0, -1)]
        kv_all = jnp.concatenate([*blocks, kv_own], axis=1)
    if swap:
        out_other, gate_other, down_other = (
            swapped(w_out), swapped(expert_gate_up), swapped(expert_down)
        )
        own_first = lax.axis_index("group") == 0
    if look_back <= 8:
        first_key = (my_block - (look_back - 1)) * rows_dev
        attended = attend_window(kv_all, first_key, query_heads, query_pos, query_start)
    else:
        soft_state = visit_block(init_state, kv_own, my_block, query_heads, query_pos, query_start)

        def cycle_turn(turn_idx, loop_state):
            moving, inner_state = loop_state
            moving = passed_along(moving, ("group", "ctx"), 1)
            return (
                moving,
                visit_block(
                    inner_state, moving, my_block - turn_idx, query_heads, query_pos, query_start
                ),
            )

        moving, soft_state = lax.fori_loop(1, look_back, cycle_turn, (kv_own, soft_state))
        run_max, run_sum, run_acc = soft_state
        attended = run_acc / run_sum[..., None]
    attended = jnp.transpose(attended, (2, 0, 1, 3)).reshape(rows_dev, -1).astype(jnp.bfloat16)
    exp_size = lax.axis_size("exp")
    exp_me = lax.axis_index("exp")
    tok_e = rows_dev // exp_size
    ahead = [(exp_me + by) % exp_size for by in range(exp_size)]
    rolled = jnp.concatenate(
        [lax.dynamic_slice_in_dim(attended, to * tok_e, tok_e, 0) for to in ahead], axis=0
    )
    if swap:
        partial = joined(own_first, matmul(rolled, w_out), matmul(rolled, out_other))
    else:
        partial = matmul(rolled, lax.all_gather(w_out, "group", axis=1, tiled=True))
    projected = summed_from(partial, exp_size, tok_e, 1)
    stream = (residual_in.astype(jnp.float32) + projected).astype(jnp.bfloat16)
    stream_f = stream.astype(jnp.float32)
    normed = (
        stream_f
        * lax.rsqrt(jnp.mean(stream_f * stream_f, axis=-1, keepdims=True) + 1e-05)
        * norm_gain
    ).astype(jnp.bfloat16)
    expert_count = router.shape[1]
    route_count = expert_ids.shape[1]
    logits = jnp.dot(normed, router, preferred_element_type=jnp.float32)
    chosen = expert_ids[:, :, None] == jnp.arange(expert_count, dtype=jnp.int32)[None, None, :]
    picked_logits = jnp.sum(jnp.where(chosen, logits[:, None, :], 0.0), axis=-1)
    raw_gates = jax.nn.sigmoid(picked_logits)
    gate_probs = raw_gates / jnp.sum(raw_gates, axis=-1, keepdims=True)
    all_normed = jnp.concatenate(
        [normed, *[turned(normed, "exp", by) for by in range(1, exp_size)]], axis=0
    )
    shared_pre = jnp.einsum(
        "td,dkf->tkf", all_normed, shared_gate_up, preferred_element_type=jnp.float32
    )
    shared_act = (jax.nn.silu(shared_pre[:, 0]) * shared_pre[:, 1]).astype(jnp.bfloat16)
    shared_out = summed_from(matmul(shared_act, shared_down), exp_size, tok_e, -1)
    slot_count = max(2, 3 * tok_e * route_count // (2 * expert_count))
    flat_ids = expert_ids.reshape(-1)
    order = jnp.arange(flat_ids.shape[0], dtype=jnp.int32)
    earlier = (flat_ids[None, :] == flat_ids[:, None]) & (order[None, :] < order[:, None])
    slot_of = jnp.sum(earlier.astype(jnp.int32), axis=1, dtype=jnp.int32)
    target = flat_ids * slot_count + slot_of
    placing = (
        jnp.arange(expert_count * slot_count, dtype=jnp.int32)[:, None] == target[None, :]
    ).astype(jnp.bfloat16)
    placing = jnp.sum(placing.reshape(expert_count * slot_count, tok_e, route_count), axis=2)
    model_width = normed.shape[1]
    outgoing = (
        jnp.dot(placing, normed, preferred_element_type=jnp.float32)
        .astype(jnp.bfloat16)
        .reshape(expert_count, slot_count, model_width)
    )
    if not swap:
        gate_up_full = lax.all_gather(expert_gate_up, "group", axis=1, tiled=True)
        down_full = lax.all_gather(expert_down, "group", axis=1, tiled=True)
    hidden_count = expert_down.shape[2]
    local_experts = expert_gate_up.shape[0]
    arrived = lax.all_to_all(outgoing, ("ctx", "exp"), split_axis=0, concat_axis=0, tiled=True)
    sources = arrived.shape[0] // local_experts
    grouped = arrived.reshape(sources, local_experts, arrived.shape[1], arrived.shape[2])
    if swap:
        half = model_width // 2
        mine = lax.dynamic_slice_in_dim(grouped, lax.axis_index("group") * half, half, 3)
        others = lax.dynamic_slice_in_dim(grouped, (1 - lax.axis_index("group")) * half, half, 3)
        pre_act = jnp.einsum(
            "nekd,edf->nekf", mine, expert_gate_up, preferred_element_type=jnp.float32
        ) + jnp.einsum("nekd,edf->nekf", others, gate_other, preferred_element_type=jnp.float32)
    else:
        pre_act = jnp.einsum(
            "nekd,edf->nekf", grouped, gate_up_full, preferred_element_type=jnp.float32
        )
    activated = (jax.nn.silu(pre_act[..., :hidden_count]) * pre_act[..., hidden_count:]).astype(
        jnp.bfloat16
    )
    def down(rows):
        return jnp.einsum(
            "nekf,edf->nekd", activated, rows, preferred_element_type=jnp.float32
        ).astype(jnp.bfloat16)

    if swap:
        result = joined(own_first, down(expert_down), down(down_other))
    else:
        result = down(down_full)
    returned = lax.all_to_all(
        result.reshape(arrived.shape), ("ctx", "exp"), split_axis=0, concat_axis=0, tiled=True
    )
    flat_back = returned.reshape(expert_count * slot_count, model_width)
    fetched = (
        jnp.take(flat_back, target, axis=0)
        .reshape(tok_e, route_count, model_width)
        .astype(jnp.float32)
    )
    routed = jnp.sum(gate_probs[:, :, None] * fetched, axis=1)
    return (stream_f + shared_out + routed).astype(jnp.bfloat16)


def solution(mesh):
    in_specs = (
        P(("group", "ctx"), "exp"),
        P(("group", "ctx"), "exp"),
        P(("group", "ctx"), "exp"),
        P(("group", "ctx", "exp"), None),
        P(),
        P("exp", "group"),
        P(),
        P(),
        P(("group", "ctx", "exp"), None),
        P(("ctx", "exp"), "group", None),
        P(("ctx", "exp"), "group", None),
        P(None, None, "exp"),
        P("exp", None),
    )
    out_specs = P(("group", "ctx", "exp"), None)
    sizes = (mesh.shape["group"], mesh.shape["ctx"], mesh.shape["exp"])
    body = with_kernels if sizes == (2, 4, 4) else on_device
    return jax.shard_map(
        body, mesh=mesh, in_specs=in_specs, out_specs=out_specs, check_vma=False
    )
```
